32 devices in a mesh: scene: 8 (over y, x, core), batch: 4 (over z).
Axes of the slice: x: 2, y: 2, z: 4, core: 2. Of those that a mesh axis runs over, the one named last changes fastest.
Arguments:
- tokens: float32 [4, 3072, 384], P('batch', 'scene'), may hold values from -6 to 6
- nbr_offset: int32 [27, 4, 3072], P(None, 'batch', 'scene'), may hold values from -64 to 65, as said below
- cotangent: float32 [4, 3072, 384], P('batch', 'scene'), may hold values from -6 to 6
- conv_weight: float32 [27, 384], replicated, may hold values from -1.25 to 1.25
- w_qkv: float32 [384, 1152], replicated, may hold values from -0.3125 to 0.3125
- w_out: float32 [384, 384], replicated, may hold values from -0.3125 to 0.3125
- score_bias: float32 [24, 32, 32], replicated, may hold values from -6 to 400
- w_up: float32 [384, 1536], replicated, may hold values from -0.3125 to 0.3125
- w_down: float32 [1536, 384], replicated, may hold values from -0.15625 to 0.15625
Outputs:
- block_out: float32 [4, 3072, 384], P('batch', 'scene')
- grad_mid: float32 [4, 3072, 384], P('batch', 'scene')
- grad_up: float32 [384, 1536], P('scene', 'batch')
- grad_down: float32 [1536, 384], P('scene', 'batch')
The draws below stay inside these ranges and needn't reach their ends.
Inputs may be any that keep to these rules, and one draw needn't show every extreme that they name: `nbr_offset`: the middle tap is 0 for every token; the value 64 + 1 marks a missing neighbour.
All inputs are finite; a program needn't handle non-finite values.
Results may differ from the reference program's by a relative error of at most 0.000075.
Values sent between devices are 32-bit elements; how exact they have to be, the bound alone decides.
A program may use at most 128 MiB of HBM per device.

```python
import jax
import jax.numpy as jnp
from jax import lax

D = 384
FF = 1536
HEADS = 24
GROUP = 32
TAPS = 27
HALO = 64
SEQ = 3072
BATCHES = 4
STRIDE = 96


def draw_nbr_offset(key, part):
    offsets = jax.random.randint(key, (TAPS, BATCHES, SEQ), -HALO, HALO + 2, dtype=jnp.int32)
    offsets = offsets.at[TAPS // 2].set(0)
    offsets = offsets.at[0, 0, 0].set(-HALO)
    offsets = offsets.at[1, 0, 0].set(HALO + 1)
    return offsets


def draw_score_bias(key, part):
    base_key = jax.random.fold_in(key, 0)
    values = jnp.clip(jax.random.normal(base_key, (HEADS, GROUP, GROUP), jnp.float32), -6.0, 6.0)
    return values


def level_of(rng, extent, shards, low, largest):
    level, own = 1.0, jax.random.fold_in(rng, 6)
    for position, shards_of in shards:
        heights = jnp.exp(jax.random.uniform(jax.random.fold_in(own, position), (shards_of,), jnp.float32, low / len(shards), largest / len(shards)))
        level = level * jnp.repeat(heights, extent[position] // shards_of).reshape([-1 if axis == position else 1 for axis in range(len(extent))])
    return level


def centred(own_key, extent, width, limit, cuts=(), held_as=jnp.bfloat16):
    entries = width * jax.random.normal(own_key, extent, jnp.float32)
    if cuts:
        entries = entries * level_of(own_key, extent, cuts, -0.22, 0.18)
    return jnp.clip(entries, -limit, limit).astype(held_as)


def setup_inputs(seed: int = 0) -> dict:
    key_of = jax.random.split(jax.random.key(seed), 10)
    tokens = centred(key_of[0], (BATCHES, SEQ, D), 1.0, 6.0, ((0, 4), (1, 8)), jnp.float32)
    nbr_offset = draw_nbr_offset(jax.random.fold_in(key_of[9], 71), 0)
    cotangent = centred(key_of[2], (BATCHES, SEQ, D), 1.0, 6.0, ((0, 4), (1, 8)), jnp.float32)
    conv_weight = centred(key_of[3], (TAPS, D), TAPS ** -0.5, 1.25, (), jnp.float32)
    w_qkv = centred(key_of[4], (D, 3 * D), D ** -0.5, 0.3125, (), jnp.float32)
    w_out = centred(key_of[5], (D, D), D ** -0.5, 0.3125, (), jnp.float32)
    score_bias = draw_score_bias(jax.random.fold_in(key_of[9], 71), 0)
    w_up = centred(key_of[7], (D, FF), D ** -0.5, 0.3125, (), jnp.float32)
    w_down = centred(key_of[8], (FF, D), FF ** -0.5, 0.15625, (), jnp.float32)
    return {"tokens": tokens, "nbr_offset": nbr_offset, "cotangent": cotangent, "conv_weight": conv_weight, "w_qkv": w_qkv, "w_out": w_out, "score_bias": score_bias, "w_up": w_up, "w_down": w_down}


def layer_norm(values):
    average = lax.optimization_barrier(jnp.mean(values, axis=-1, keepdims=True))
    centered = values - average
    variance = lax.optimization_barrier(jnp.mean(centered * centered, axis=-1, keepdims=True))
    return centered * lax.rsqrt(variance + 1e-05)

def group_attention(members, score_bias):
    count, slots, channels = members.shape
    feature_width = channels // 3
    head_count = score_bias.shape[0]
    head_dim = feature_width // head_count
    query = members[:, :, :feature_width].reshape(count, slots, head_count, head_dim)
    keys = members[:, :, feature_width:2 * feature_width].reshape(count, slots, head_count, head_dim)
    values = members[:, :, 2 * feature_width:].reshape(count, slots, head_count, head_dim)
    scores = jnp.einsum('nihd,njhd->nhij', query, keys, precision=lax.Precision.HIGHEST) * head_dim ** (-0.5)
    scores = scores + score_bias[None]
    weights = jax.nn.softmax(scores, axis=-1)
    mixed = jnp.einsum('nhij,njhd->nihd', weights, values, precision=lax.Precision.HIGHEST)
    return mixed.reshape(count, slots, feature_width)

def mlp_branch(middle, w_up, w_down):
    normed = layer_norm(middle)
    hidden = jnp.dot(normed, w_up, precision=lax.Precision.HIGHEST, preferred_element_type=jnp.float32)
    activation = jax.nn.gelu(hidden, approximate=False)
    return middle + jnp.dot(activation, w_down, precision=lax.Precision.HIGHEST, preferred_element_type=jnp.float32)

def reference(tokens, nbr_offset, cotangent, conv_weight, w_qkv, w_out, score_bias, w_up, w_down):
    feature_width = tokens.shape[2]
    positions = jnp.arange(SEQ, dtype=jnp.int32)
    padded = jnp.pad(tokens, ((0, 0), (HALO, HALO + 1), (0, 0)))
    stencil = jnp.zeros_like(tokens)
    for tap_index in range(TAPS):
        offsets = nbr_offset[tap_index]
        row_index = jnp.where(offsets > HALO, SEQ + 2 * HALO, positions[None, :] + HALO + offsets).astype(jnp.int32)
        picked = jax.vmap(lambda table, where_rows: table[where_rows])(padded, row_index)
        stencil = stencil + picked * conv_weight[tap_index]
    first = tokens + stencil
    normed = layer_norm(first).reshape(BATCHES * SEQ, feature_width)
    qkv = jnp.dot(normed, w_qkv, precision=lax.Precision.HIGHEST, preferred_element_type=jnp.float32)
    grouped = qkv.reshape(BATCHES, GROUP, STRIDE, 3 * feature_width).transpose(0, 2, 1, 3)
    grouped = grouped.reshape(BATCHES * STRIDE, GROUP, 3 * feature_width)
    attended = group_attention(grouped, score_bias)
    attended = attended.reshape(BATCHES, STRIDE, GROUP, feature_width).transpose(0, 2, 1, 3)
    attended = attended.reshape(BATCHES * SEQ, feature_width)
    middle = first.reshape(BATCHES * SEQ, feature_width) + jnp.dot(attended, w_out, precision=lax.Precision.HIGHEST, preferred_element_type=jnp.float32)
    block_out, pullback = jax.vjp(mlp_branch, middle, w_up, w_down)
    grad_mid, grad_up, grad_down = pullback(cotangent.reshape(BATCHES * SEQ, feature_width))
    grad_scale = lax.rsqrt(jnp.asarray(BATCHES * SEQ, jnp.float32))
    return (block_out.reshape(BATCHES, SEQ, feature_width), grad_mid.reshape(BATCHES, SEQ, feature_width), grad_up * grad_scale, grad_down * grad_scale)
```

```python
import functools

import jax
import jax.numpy as jnp
import numpy as np
from jax import lax
from jax.experimental import pallas as pl
from jax.experimental.pallas import tpu as pltpu
from jax.sharding import PartitionSpec as P

GROUP = 32
HALO = 64
TILE = 128
F32 = jnp.float32
BF16 = jnp.bfloat16
VMEM_LIMIT = 56 * 1024 * 1024


def split(x):
    hi = x.astype(BF16)
    return hi, (x - hi.astype(F32)).astype(BF16)


def left3(x, axis=1):
    hi, lo = split(x)
    return jnp.concatenate([hi, hi, lo], axis=axis)


def right3(x, axis=0):
    hi, lo = split(x)
    return jnp.concatenate([hi, lo, hi], axis=axis)


def dot(a, b):
    return lax.dot_general(a, b, (((1,), (0,)), ((), ())), preferred_element_type=F32)


def dot_t(a, b):
    return lax.dot_general(a, b, (((1,), (1,)), ((), ())), preferred_element_type=F32)


def norm_of(values):
    average = jnp.mean(values, axis=-1, keepdims=True)
    centered = values - average
    variance = jnp.mean(centered * centered, axis=-1, keepdims=True)
    scale = lax.rsqrt(variance + 1e-05)
    return centered * scale, scale


def conv_kernel(local_ref, low_ref, high_ref, offset_ref, weight_ref, first_ref, normed_ref, ext, off_t):
    tok, width = local_ref.shape
    taps = weight_ref.shape[0]
    for start, ref in ((0, low_ref), (HALO, local_ref), (HALO + tok, high_ref)):
        hi, lo = split(ref[...])
        ext[pl.ds(start, ref.shape[0]), :width] = hi
        ext[pl.ds(start, ref.shape[0]), width:] = lo
    for b in range(tok // TILE):
        piece = offset_ref[:, b * TILE : (b + 1) * TILE]
        piece = jnp.where(piece > HALO, 4 * TILE, piece).astype(F32)
        piece = jnp.concatenate([piece, jnp.zeros((TILE - taps, TILE), F32)], axis=0)
        off_t[b * TILE : (b + 1) * TILE, :] = piece.T
    span = TILE + 2 * HALO
    base = (
        lax.broadcasted_iota(jnp.int32, (TILE, span), 1)
        - lax.broadcasted_iota(jnp.int32, (TILE, span), 0)
        - HALO
    ).astype(F32)

    @pl.loop(0, tok // TILE)
    def _(b):
        row = pl.multiple_of(b * TILE, TILE)
        window = ext[pl.ds(row, span), :]
        offsets = off_t[pl.ds(row, TILE), :]
        total = local_ref[pl.ds(row, TILE), :]
        for a in range(taps):
            pick = jnp.where(base == offsets[:, a : a + 1], 1.0, 0.0).astype(BF16)
            found = dot(pick, window)
            total += (found[:, :width] + found[:, width:]) * weight_ref[a : a + 1, :]
        first_ref[pl.ds(row, TILE), :] = total
        normed_ref[pl.ds(row, TILE), :] = norm_of(total)[0]


def attend_kernel(head_dim, x_ref, perm_ref, back_ref, wqkv_ref, wout_ref, bias_ref, out_ref, qkv, att):
    tok, width = x_ref.shape
    hi, lo = split(x_ref[...])
    hi = dot(perm_ref[...], hi).astype(BF16)
    lo = dot(perm_ref[...], lo).astype(BF16)
    rows3 = jnp.concatenate([hi, hi, lo], axis=1)
    for part in range(3):
        qkv[:, part * width : (part + 1) * width] = dot(
            rows3, right3(wqkv_ref[:, part * width : (part + 1) * width])
        )
    per_lane = TILE // head_dim
    shape = (TILE, TILE)
    same = (lax.broadcasted_iota(jnp.int32, shape, 0) ^ lax.broadcasted_iota(jnp.int32, shape, 1)) < GROUP
    away = jnp.where(same, 0.0, -1e30)
    lane = lax.broadcasted_iota(jnp.int32, shape, 1)

    @pl.loop(0, tok // TILE)
    def _(b):
        row = pl.ds(pl.multiple_of(b * TILE, TILE), TILE)
        for part in range(width // TILE):
            at = part * TILE
            q = qkv[row, at : at + TILE] * (head_dim**-0.5)
            k = qkv[row, width + at : width + at + TILE]
            v = qkv[row, 2 * width + at : 2 * width + at + TILE]
            keys, values = [], []
            for h in range(per_lane):
                mine = (lane >= h * head_dim) & (lane < (h + 1) * head_dim)
                keys.append(right3(jnp.where(mine, k, 0.0), axis=1))
                values.append(jnp.concatenate(split(jnp.where(mine, v, 0.0)), axis=1))
            scores = dot_t(left3(q), jnp.concatenate(keys, axis=0))
            his, los = [], []
            for h in range(per_lane):
                bias = jnp.concatenate([bias_ref[part * per_lane + h]] * (TILE // GROUP), axis=0)
                s = scores[:, h * TILE : (h + 1) * TILE] + bias + away
                e = jnp.exp(s - jnp.max(s, axis=-1, keepdims=True))
                p = e / jnp.sum(e, axis=-1, keepdims=True)
                p_hi, p_lo = split(p)
                his.append(p_hi)
                los.append(p_lo)
            values = jnp.concatenate(values, axis=0)
            both = dot(jnp.concatenate(his, axis=1), values)
            rest = dot(jnp.concatenate(los, axis=1), values[:, :TILE])
            att[row, at : at + TILE] = both[:, :TILE] + both[:, TILE:] + rest

    hi, lo = split(att[...])
    hi = dot(back_ref[...], hi).astype(BF16)
    lo = dot(back_ref[...], lo).astype(BF16)
    out_ref[...] = dot(jnp.concatenate([hi, hi, lo], axis=1), right3(wout_ref[...]))


def mlp_kernel(
    grad_scale, first_ref, mixed_ref, cot_ref, up_ref, down_ref,
    out_ref, mid_ref, gup_ref, gdown_ref,
    n_left, c_left, nt_left, ct_left, grad_normed,
):
    tok, width = first_ref.shape
    hidden_width = up_ref.shape[1]
    chunk = 2 * TILE
    middle = first_ref[...] + mixed_ref[...]
    normed, scale = norm_of(middle)
    cot = cot_ref[...]
    n_left[...] = left3(normed)
    c_left[...] = left3(cot)
    nt_left[...] = left3(normed.T * grad_scale)
    ct_left[...] = left3(cot.T * grad_scale)
    out_ref[...] = middle
    grad_normed[...] = jnp.zeros_like(grad_normed)

    @pl.loop(0, hidden_width // chunk)
    def _(c):
        at = pl.ds(pl.multiple_of(c * chunk, chunk), chunk)
        up_hi, up_lo = split(up_ref[:, at])
        down_hi, down_lo = split(down_ref[at, :])
        hidden = dot(n_left[...], jnp.concatenate([up_hi, up_lo, up_hi], axis=0))
        grad_act = dot_t(c_left[...], jnp.concatenate([down_hi, down_lo, down_hi], axis=1))
        cdf = 0.5 * (1.0 + lax.erf(hidden * (0.5**0.5)))
        act = hidden * cdf
        density = jnp.exp(-0.5 * hidden * hidden) * ((2.0 * np.pi) ** -0.5)
        grad_hidden = grad_act * (cdf + hidden * density)
        act_hi, act_lo = split(act)
        gh_hi, gh_lo = split(grad_hidden)
        gup_ref[:, at] = dot(nt_left[...], jnp.concatenate([gh_hi, gh_lo, gh_hi], axis=0))
        gdown_ref[at, :] = dot(ct_left[...], jnp.concatenate([act_hi, act_lo, act_hi], axis=0)).T
        out_ref[...] += dot(
            jnp.concatenate([act_hi, act_hi, act_lo], axis=1),
            jnp.concatenate([down_hi, down_lo, down_hi], axis=0),
        )
        grad_normed[...] += dot_t(
            jnp.concatenate([gh_hi, gh_hi, gh_lo], axis=1),
            jnp.concatenate([up_hi, up_lo, up_hi], axis=1),
        )

    g = grad_normed[...]
    along = jnp.mean(g * normed, axis=-1, keepdims=True)
    mid_ref[...] = cot + scale * (g - jnp.mean(g, axis=-1, keepdims=True) - normed * along)


def shape_of(*dims):
    return jax.ShapeDtypeStruct(dims, F32)


def call(kernel, outs, scratch, flops):
    return pl.pallas_call(
        kernel,
        out_shape=outs,
        scratch_shapes=scratch,
        compiler_params=pltpu.CompilerParams(vmem_limit_bytes=VMEM_LIMIT),
        cost_estimate=pl.CostEstimate(flops=flops, bytes_accessed=4000000, transcendentals=0),
    )


def orders(tok, scene_count):
    per, count = GROUP // scene_count, tok // GROUP
    row = np.arange(tok)
    group, slot = row // GROUP, row % GROUP
    source = ((slot % per) * scene_count + slot // per) * count + group
    perm = np.zeros((tok, tok), np.float32)
    perm[row, source] = 1.0
    return perm


def on_device(tokens, nbr_offset, cotangent, conv_weight, w_qkv, w_out, score_bias, w_up, w_down):
    local = tokens[0]
    tok, width = local.shape
    hidden_width = w_up.shape[1]
    heads = score_bias.shape[0]
    scene_count = lax.axis_size("scene")
    batch_count = lax.axis_size("batch")
    forward = [(i, i + 1) for i in range(scene_count - 1)]
    backward = [(target, source) for source, target in forward]
    low = lax.ppermute(local[tok - HALO :], "scene", forward)
    high = lax.ppermute(local[:HALO], "scene", backward)
    first, normed = call(
        conv_kernel,
        (shape_of(tok, width), shape_of(tok, width)),
        [pltpu.VMEM((tok + 2 * HALO, 2 * width), BF16), pltpu.VMEM((tok, TILE), F32)],
        8 * 10**9,
    )(local, low, high, nbr_offset[:, 0, :], conv_weight)
    per, count = GROUP // scene_count, tok // GROUP
    blocks = normed.reshape(per, scene_count, count, width)
    arrived = lax.all_to_all(blocks, "scene", split_axis=1, concat_axis=1, tiled=True)
    perm = orders(tok, scene_count)
    bias = jnp.tile(score_bias, (1, 1, TILE // GROUP))
    mixed = call(
        functools.partial(attend_kernel, width // heads),
        shape_of(tok, width),
        [pltpu.VMEM((tok, 3 * width), F32), pltpu.VMEM((tok, width), F32)],
        10**10,
    )(
        arrived.reshape(tok, width),
        jnp.asarray(perm, BF16),
        jnp.asarray(perm.T, BF16),
        w_qkv,
        w_out,
        bias,
    )
    returned = lax.all_to_all(
        mixed.reshape(per, scene_count, count, width), "scene", split_axis=1, concat_axis=1, tiled=True
    ).reshape(tok, width)
    grad_scale = float(tok * scene_count * batch_count) ** -0.5
    block_out, grad_mid, grad_up, grad_down = call(
        functools.partial(mlp_kernel, grad_scale),
        (
            shape_of(tok, width),
            shape_of(tok, width),
            shape_of(width, hidden_width),
            shape_of(hidden_width, width),
        ),
        [pltpu.VMEM((tok, 3 * width), BF16)] * 2
        + [pltpu.VMEM((width, 3 * tok), BF16)] * 2
        + [pltpu.VMEM((tok, width), F32)],
        10**10,
    )(first, returned, cotangent[0], w_up, w_down)
    grads = []
    for grad in (grad_up, grad_down):
        part = lax.psum_scatter(grad, "scene", scatter_dimension=0, tiled=True)
        grads.append(lax.psum_scatter(part, "batch", scatter_dimension=1, tiled=True))
    return (block_out[None], grad_mid[None], *grads)


def solution(mesh):
    tokens = P("batch", "scene", None)
    return jax.shard_map(
        on_device,
        mesh=mesh,
        in_specs=(tokens, P(None, "batch", "scene"), tokens) + (P(),) * 6,
        out_specs=(tokens, tokens, P("scene", "batch"), P("scene", "batch")),
        check_vma=False,
    )
```

```python
import functools

import jax
import jax.numpy as jnp
import numpy as np
from jax import lax
from jax.experimental import pallas as pl
from jax.experimental.pallas import tpu as pltpu
from jax.sharding import PartitionSpec as P

GROUP = 32
HALO = 64
TILE = 128
F32 = jnp.float32
BF16 = jnp.bfloat16
MESH = pl.DeviceIdType.MESH
VMEM_LIMIT = 56 * 1024 * 1024


def split(x):
    hi = x.astype(BF16)
    return hi, (x - hi.astype(F32)).astype(BF16)


def left3(x, axis=1):
    hi, lo = split(x)
    return jnp.concatenate([hi, hi, lo], axis=axis)


def right3(x, axis=0):
    hi, lo = split(x)
    return jnp.concatenate([hi, lo, hi], axis=axis)


def dot(a, b):
    return lax.dot_general(a, b, (((1,), (0,)), ((), ())), preferred_element_type=F32)


def dot_t(a, b):
    return lax.dot_general(a, b, (((1,), (1,)), ((), ())), preferred_element_type=F32)


def norm_of(values):
    average = jnp.mean(values, axis=-1, keepdims=True)
    centered = values - average
    variance = jnp.mean(centered * centered, axis=-1, keepdims=True)
    scale = lax.rsqrt(variance + 1e-05)
    return centered * scale, scale


def conv_kernel(local_ref, low_ref, high_ref, offset_ref, weight_ref, first_ref, normed_ref, ext, off_t):
    tok, width = local_ref.shape
    taps = weight_ref.shape[0]
    for start, ref in ((0, low_ref), (HALO, local_ref), (HALO + tok, high_ref)):
        hi, lo = split(ref[...])
        ext[pl.ds(start, ref.shape[0]), :width] = hi
        ext[pl.ds(start, ref.shape[0]), width:] = lo
    for b in range(tok // TILE):
        piece = offset_ref[:, b * TILE : (b + 1) * TILE]
        piece = jnp.where(piece > HALO, 4 * TILE, piece).astype(F32)
        piece = jnp.concatenate([piece, jnp.zeros((TILE - taps, TILE), F32)], axis=0)
        off_t[b * TILE : (b + 1) * TILE, :] = piece.T
    span = TILE + 2 * HALO
    base = (
        lax.broadcasted_iota(jnp.int32, (TILE, span), 1)
        - lax.broadcasted_iota(jnp.int32, (TILE, span), 0)
        - HALO
    ).astype(F32)

    @pl.loop(0, tok // TILE)
    def _(b):
        row = pl.multiple_of(b * TILE, TILE)
        window = ext[pl.ds(row, span), :]
        offsets = off_t[pl.ds(row, TILE), :]
        total = local_ref[pl.ds(row, TILE), :]
        for a in range(taps):
            pick = jnp.where(base == offsets[:, a : a + 1], 1.0, 0.0).astype(BF16)
            found = dot(pick, window)
            total += (found[:, :width] + found[:, width:]) * weight_ref[a : a + 1, :]
        first_ref[pl.ds(row, TILE), :] = total
        normed_ref[pl.ds(row, TILE), :] = norm_of(total)[0]


def attend_kernel(head_dim, x_ref, perm_ref, back_ref, wqkv_ref, wout_ref, bias_ref, out_ref, qkv, att):
    tok, width = x_ref.shape
    hi, lo = split(x_ref[...])
    hi = dot(perm_ref[...], hi).astype(BF16)
    lo = dot(perm_ref[...], lo).astype(BF16)
    rows3 = jnp.concatenate([hi, hi, lo], axis=1)
    for part in range(3):
        qkv[:, part * width : (part + 1) * width] = dot(
            rows3, right3(wqkv_ref[:, part * width : (part + 1) * width])
        )
    per_lane = TILE // head_dim
    shape = (TILE, TILE)
    same = (lax.broadcasted_iota(jnp.int32, shape, 0) ^ lax.broadcasted_iota(jnp.int32, shape, 1)) < GROUP
    away = jnp.where(same, 0.0, -1e30)
    lane = lax.broadcasted_iota(jnp.int32, shape, 1)

    @pl.loop(0, tok // TILE)
    def _(b):
        row = pl.ds(pl.multiple_of(b * TILE, TILE), TILE)
        for part in range(width // TILE):
            at = part * TILE
            q = qkv[row, at : at + TILE] * (head_dim**-0.5)
            k = qkv[row, width + at : width + at + TILE]
            v = qkv[row, 2 * width + at : 2 * width + at + TILE]
            keys, values = [], []
            for h in range(per_lane):
                mine = (lane >= h * head_dim) & (lane < (h + 1) * head_dim)
                keys.append(right3(jnp.where(mine, k, 0.0), axis=1))
                values.append(jnp.concatenate(split(jnp.where(mine, v, 0.0)), axis=1))
            scores = dot_t(left3(q), jnp.concatenate(keys, axis=0))
            his, los = [], []
            for h in range(per_lane):
                bias = jnp.concatenate([bias_ref[part * per_lane + h]] * (TILE // GROUP), axis=0)
                s = scores[:, h * TILE : (h + 1) * TILE] + bias + away
                e = jnp.exp(s - jnp.max(s, axis=-1, keepdims=True))
                p = e / jnp.sum(e, axis=-1, keepdims=True)
                p_hi, p_lo = split(p)
                his.append(p_hi)
                los.append(p_lo)
            values = jnp.concatenate(values, axis=0)
            both = dot(jnp.concatenate(his, axis=1), values)
            rest = dot(jnp.concatenate(los, axis=1), values[:, :TILE])
            att[row, at : at + TILE] = both[:, :TILE] + both[:, TILE:] + rest

    hi, lo = split(att[...])
    hi = dot(back_ref[...], hi).astype(BF16)
    lo = dot(back_ref[...], lo).astype(BF16)
    out_ref[...] = dot(jnp.concatenate([hi, hi, lo], axis=1), right3(wout_ref[...]))


def mlp_kernel(
    grad_scale, first_ref, mixed_ref, cot_ref, up_ref, down_ref,
    out_ref, mid_ref, gup_ref, gdown_ref,
    n_left, c_left, nt_left, ct_left, grad_normed,
):
    tok, width = first_ref.shape
    hidden_width = up_ref.shape[1]
    chunk = 2 * TILE
    middle = first_ref[...] + mixed_ref[...]
    normed, scale = norm_of(middle)
    cot = cot_ref[...]
    n_left[...] = left3(normed)
    c_left[...] = left3(cot)
    nt_left[...] = left3(normed.T * grad_scale)
    ct_left[...] = left3(cot.T * grad_scale)
    out_ref[...] = middle
    grad_normed[...] = jnp.zeros_like(grad_normed)

    @pl.loop(0, hidden_width // chunk)
    def _(c):
        at = pl.ds(pl.multiple_of(c * chunk, chunk), chunk)
        up_hi, up_lo = split(up_ref[:, at])
        down_hi, down_lo = split(down_ref[at, :])
        hidden = dot(n_left[...], jnp.concatenate([up_hi, up_lo, up_hi], axis=0))
        grad_act = dot_t(c_left[...], jnp.concatenate([down_hi, down_lo, down_hi], axis=1))
        cdf = 0.5 * (1.0 + lax.erf(hidden * (0.5**0.5)))
        act = hidden * cdf
        density = jnp.exp(-0.5 * hidden * hidden) * ((2.0 * np.pi) ** -0.5)
        grad_hidden = grad_act * (cdf + hidden * density)
        act_hi, act_lo = split(act)
        gh_hi, gh_lo = split(grad_hidden)
        gup_ref[:, at] = dot(nt_left[...], jnp.concatenate([gh_hi, gh_lo, gh_hi], axis=0))
        gdown_ref[at, :] = dot(ct_left[...], jnp.concatenate([act_hi, act_lo, act_hi], axis=0)).T
        out_ref[...] += dot(
            jnp.concatenate([act_hi, act_hi, act_lo], axis=1),
            jnp.concatenate([down_hi, down_lo, down_hi], axis=0),
        )
        grad_normed[...] += dot_t(
            jnp.concatenate([gh_hi, gh_hi, gh_lo], axis=1),
            jnp.concatenate([up_hi, up_lo, up_hi], axis=1),
        )

    g = grad_normed[...]
    along = jnp.mean(g * normed, axis=-1, keepdims=True)
    mid_ref[...] = cot + scale * (g - jnp.mean(g, axis=-1, keepdims=True) - normed * along)


def bits_of(index, order):
    return tuple((index >> bit) & 1 for bit in order)


def mlp_reduce_kernel(
    grad_scale, orders_ab, batch_count,
    first_ref, mixed_ref, cot_ref, up_ref, down_ref,
    out_ref, mid_ref, gup_ref, gdown_ref,
    n_left, c_left, nt_left, ct_left, slope, act_hi, act_lo, gh_hi, gh_lo,
    acc_a, acc_b, recv_a, recv_b, zrecv_a, zsend_b, zrecv_b,
    send_sem, recv_sem, za_send, za_recv, zb_send, zb_recv,
):
    tok, width = first_ref.shape
    hidden_width = up_ref.shape[1]
    steps = len(orders_ab[0])
    scene_count = 2**steps
    rows_a, rows_b = width // scene_count, hidden_width // scene_count
    cols_a, cols_b = hidden_width // batch_count, width // batch_count
    pieces_a, pieces_b = cols_a // TILE, width // TILE
    me, my_batch = lax.axis_index("scene"), lax.axis_index("batch")
    values = [(me // 2**bit) % 2 for bit in range(steps)]
    partners = [me + (1 - 2 * values[bit]) * 2**bit for bit in range(steps)]
    others = [lax.rem(my_batch + d, batch_count) for d in range(1, batch_count)]

    barrier = pltpu.get_barrier_semaphore()
    for partner in partners:
        pl.semaphore_signal(barrier, inc=1, device_id={"scene": partner}, device_id_type=MESH)
    for other in others:
        pl.semaphore_signal(barrier, inc=1, device_id={"batch": other}, device_id_type=MESH)

    accs, recvs = (acc_a, acc_b), (recv_a, recv_b)
    sent = []

    def kept(stream, upto):
        return tuple(values[bit] for bit in orders_ab[stream][:upto])

    def halving(stream, q, i):
        bit = orders_ab[stream][i]
        return pltpu.make_async_remote_copy(
            src_ref=accs[stream].at[(q, *kept(stream, i), 1 - values[bit])],
            dst_ref=recvs[stream][i].at[q],
            send_sem=send_sem.at[stream, q, i],
            recv_sem=recv_sem.at[stream, q, i],
            device_id={"scene": partners[bit]},
            device_id_type=MESH,
        )

    def start(copy):
        copy.start()
        sent.append(copy)

    def z_a(q, d):
        return pltpu.make_async_remote_copy(
            src_ref=acc_a.at[(q, *kept(0, steps), others[d])],
            dst_ref=zrecv_a.at[q, d],
            send_sem=za_send.at[q, d],
            recv_sem=za_recv.at[q, d],
            device_id={"batch": others[d]},
            device_id_type=MESH,
        )

    def z_b(d):
        return pltpu.make_async_remote_copy(
            src_ref=zsend_b.at[others[d]],
            dst_ref=zrecv_b.at[d],
            send_sem=zb_send.at[d],
            recv_sem=zb_recv.at[d],
            device_id={"batch": others[d]},
            device_id_type=MESH,
        )

    def advance(stream, q, i):
        halving(stream, q, i).wait_recv()
        mine = (q, *kept(stream, i + 1))
        accs[stream][mine] = accs[stream][mine] + recvs[stream][i][q]
        if i + 1 < steps:
            start(halving(stream, q, i + 1))
        elif stream == 0:
            for d in range(batch_count - 1):
                start(z_a(q, d))
        elif q == pieces_b - 1:
            whole = jnp.concatenate([acc_b[(p, *kept(1, steps))] for p in range(pieces_b)], axis=1)
            pad = zsend_b.shape[2] - rows_b
            whole = jnp.concatenate([whole, jnp.zeros((pad, width), F32)], axis=0)
            zsend_b[...] = whole.T.reshape(zsend_b.shape)
            for d in range(batch_count - 1):
                start(z_b(d))

    middle = first_ref[...] + mixed_ref[...]
    normed, scale = norm_of(middle)
    cot = cot_ref[...]
    n_left[...] = left3(normed)
    c_left[...] = left3(cot)
    nt_left[...] = left3(normed.T * grad_scale)
    ct_left[...] = left3(cot.T * grad_scale)

    chunk = 2 * rows_b
    for c in range(hidden_width // chunk):
        at = slice(c * chunk, (c + 1) * chunk)
        hidden = dot(n_left[...], right3(up_ref[:, at]))
        cdf = 0.5 * (1.0 + lax.erf(hidden * (0.5**0.5)))
        density = jnp.exp(-0.5 * hidden * hidden) * ((2.0 * np.pi) ** -0.5)
        slope[:, at] = cdf + hidden * density
        hi, lo = split(hidden * cdf)
        act_hi[:, at] = hi
        act_lo[:, at] = lo
        grad = dot(ct_left[...], jnp.concatenate([hi, lo, hi], axis=0)).T
        for half in range(2):
            block = bits_of(2 * c + half, orders_ab[1])
            for q in range(pieces_b):
                acc_b[(q, *block)] = grad[half * rows_b : (half + 1) * rows_b, q * TILE : (q + 1) * TILE]

    pl.semaphore_wait(barrier, steps + batch_count - 1)
    for q in range(pieces_b):
        start(halving(1, q, 0))

    part = batch_count * TILE
    for q in range(pieces_a):
        where = [slice(b * cols_a + q * TILE, b * cols_a + (q + 1) * TILE) for b in range(batch_count)]
        down = jnp.concatenate([down_ref[w, :] for w in where], axis=0)
        grad_act = dot_t(c_left[...], right3(down, axis=1))
        hi, lo = split(grad_act * jnp.concatenate([slope[:, w] for w in where], axis=1))
        gh_hi[:, q * part : (q + 1) * part] = hi
        gh_lo[:, q * part : (q + 1) * part] = lo
        grad = dot(nt_left[...], jnp.concatenate([hi, lo, hi], axis=0))
        for s in range(scene_count):
            for b in range(batch_count):
                acc_a[(q, *bits_of(s, orders_ab[0]), b)] = grad[
                    s * rows_a : (s + 1) * rows_a, b * TILE : (b + 1) * TILE
                ]
        start(halving(0, q, 0))
        if q == 0:
            for p in range(pieces_b):
                advance(1, p, 0)
        else:
            advance(0, q - 1, 0)

    down_hi, down_lo = split(down_ref[...])
    out_ref[...] = (
        middle + dot(act_hi[...], down_hi) + dot(act_hi[...], down_lo) + dot(act_lo[...], down_hi)
    )
    advance(0, pieces_a - 1, 0)
    advance(1, 0, 1)
    advance(0, 0, 1)

    g = jnp.zeros((tok, width), F32)
    for q in range(pieces_a):
        where = [slice(b * cols_a + q * TILE, b * cols_a + (q + 1) * TILE) for b in range(batch_count)]
        up_hi, up_lo = split(jnp.concatenate([up_ref[:, w] for w in where], axis=1))
        hi, lo = gh_hi[:, q * part : (q + 1) * part], gh_lo[:, q * part : (q + 1) * part]
        g += dot_t(hi, up_hi) + dot_t(hi, up_lo) + dot_t(lo, up_hi)
    along = jnp.mean(g * normed, axis=-1, keepdims=True)
    mid_ref[...] = cot + scale * (g - jnp.mean(g, axis=-1, keepdims=True) - normed * along)

    for i in range(1, steps):
        for q in range(max(pieces_a, pieces_b)):
            for stream, count in ((1, pieces_b), (0, pieces_a)):
                if q < count and not (i == 1 and q == 0):
                    advance(stream, q, i)
    for q in range(pieces_a):
        total = acc_a[(q, *kept(0, steps), my_batch)]
        for d in range(batch_count - 1):
            z_a(q, d).wait_recv()
            total += zrecv_a[q, d]
        gup_ref[:, q * TILE : (q + 1) * TILE] = total
    total = zsend_b[my_batch]
    for d in range(batch_count - 1):
        z_b(d).wait_recv()
        total += zrecv_b[d]
    total = jnp.concatenate([total, jnp.zeros((TILE - cols_b, total.shape[1]), F32)], axis=0)
    gdown_ref[...] = total.T[:rows_b, :cols_b]
    for copy in sent:
        copy.wait_send()


def can_fuse(width, hidden_width, scene_count, batch_count):
    return (
        scene_count >= 4
        and scene_count & (scene_count - 1) == 0
        and batch_count > 1
        and width % TILE == 0
        and (width // scene_count) % 8 == 0
        and (hidden_width // scene_count) % 64 == 0
        and (hidden_width // batch_count) % TILE == 0
        and (width // batch_count) % 8 == 0
        and width // batch_count <= TILE
    )


def mlp_reduced(grad_scale, scene_count, batch_count, first, returned, cot, w_up, w_down):
    tok, width = first.shape
    hidden_width = w_up.shape[1]
    steps = scene_count.bit_length() - 1
    orders_ab = (tuple(range(steps)), (0, *reversed(range(1, steps))))
    rows_a, rows_b = width // scene_count, hidden_width // scene_count
    cols_a, cols_b = hidden_width // batch_count, width // batch_count
    pieces_a, pieces_b = cols_a // TILE, width // TILE
    tail_a, tail_b = (batch_count, rows_a, TILE), (rows_b, TILE)
    padded = -(-rows_b // TILE) * TILE
    pieces = max(pieces_a, pieces_b)
    scratch = (
        [pltpu.VMEM((tok, 3 * width), BF16)] * 2
        + [pltpu.VMEM((width, 3 * tok), BF16)] * 2
        + [pltpu.VMEM((tok, hidden_width), F32)]
        + [pltpu.VMEM((tok, hidden_width), BF16)] * 4
        + [
            pltpu.VMEM((pieces_a, *(2,) * steps, *tail_a), F32),
            pltpu.VMEM((pieces_b, *(2,) * steps, *tail_b), F32),
            [pltpu.VMEM((pieces_a, *(2,) * (steps - 1 - i), *tail_a), F32) for i in range(steps)],
            [pltpu.VMEM((pieces_b, *(2,) * (steps - 1 - i), *tail_b), F32) for i in range(steps)],
            pltpu.VMEM((pieces_a, batch_count - 1, rows_a, TILE), F32),
            pltpu.VMEM((batch_count, cols_b, padded), F32),
            pltpu.VMEM((batch_count - 1, cols_b, padded), F32),
        ]
        + [pltpu.SemaphoreType.DMA((2, pieces, steps))] * 2
        + [pltpu.SemaphoreType.DMA((pieces_a, batch_count - 1))] * 2
        + [pltpu.SemaphoreType.DMA((batch_count - 1,))] * 2
    )
    return pl.pallas_call(
        functools.partial(mlp_reduce_kernel, grad_scale, orders_ab, batch_count),
        out_shape=(
            shape_of(tok, width),
            shape_of(tok, width),
            shape_of(rows_a, cols_a),
            shape_of(rows_b, cols_b),
        ),
        scratch_shapes=scratch,
        compiler_params=pltpu.CompilerParams(
            vmem_limit_bytes=VMEM_LIMIT, collective_id=0, has_side_effects=True
        ),
        cost_estimate=pl.CostEstimate(flops=10**10, bytes_accessed=4000000, transcendentals=0),
    )(first, returned, cot, w_up, w_down)


def shape_of(*dims):
    return jax.ShapeDtypeStruct(dims, F32)


def call(kernel, outs, scratch, flops):
    return pl.pallas_call(
        kernel,
        out_shape=outs,
        scratch_shapes=scratch,
        compiler_params=pltpu.CompilerParams(vmem_limit_bytes=VMEM_LIMIT),
        cost_estimate=pl.CostEstimate(flops=flops, bytes_accessed=4000000, transcendentals=0),
    )


def orders(tok, scene_count):
    per, count = GROUP // scene_count, tok // GROUP
    row = np.arange(tok)
    group, slot = row // GROUP, row % GROUP
    source = ((slot % per) * scene_count + slot // per) * count + group
    perm = np.zeros((tok, tok), np.float32)
    perm[row, source] = 1.0
    return perm


def on_device(tokens, nbr_offset, cotangent, conv_weight, w_qkv, w_out, score_bias, w_up, w_down):
    local = tokens[0]
    tok, width = local.shape
    hidden_width = w_up.shape[1]
    heads = score_bias.shape[0]
    scene_count = lax.axis_size("scene")
    batch_count = lax.axis_size("batch")
    forward = [(i, i + 1) for i in range(scene_count - 1)]
    backward = [(target, source) for source, target in forward]
    low = lax.ppermute(local[tok - HALO :], "scene", forward)
    high = lax.ppermute(local[:HALO], "scene", backward)
    first, normed = call(
        conv_kernel,
        (shape_of(tok, width), shape_of(tok, width)),
        [pltpu.VMEM((tok + 2 * HALO, 2 * width), BF16), pltpu.VMEM((tok, TILE), F32)],
        8 * 10**9,
    )(local, low, high, nbr_offset[:, 0, :], conv_weight)
    per, count = GROUP // scene_count, tok // GROUP
    blocks = normed.reshape(per, scene_count, count, width)
    arrived = lax.all_to_all(blocks, "scene", split_axis=1, concat_axis=1, tiled=True)
    perm = orders(tok, scene_count)
    bias = jnp.tile(score_bias, (1, 1, TILE // GROUP))
    mixed = call(
        functools.partial(attend_kernel, width // heads),
        shape_of(tok, width),
        [pltpu.VMEM((tok, 3 * width), F32), pltpu.VMEM((tok, width), F32)],
        10**10,
    )(
        arrived.reshape(tok, width),
        jnp.asarray(perm, BF16),
        jnp.asarray(perm.T, BF16),
        w_qkv,
        w_out,
        bias,
    )
    returned = lax.all_to_all(
        mixed.reshape(per, scene_count, count, width), "scene", split_axis=1, concat_axis=1, tiled=True
    ).reshape(tok, width)
    grad_scale = float(tok * scene_count * batch_count) ** -0.5
    if can_fuse(width, hidden_width, scene_count, batch_count):
        block_out, grad_mid, *grads = mlp_reduced(
            grad_scale, scene_count, batch_count, first, returned, cotangent[0], w_up, w_down
        )
        return (block_out[None], grad_mid[None], *grads)
    block_out, grad_mid, grad_up, grad_down = call(
        functools.partial(mlp_kernel, grad_scale),
        (
            shape_of(tok, width),
            shape_of(tok, width),
            shape_of(width, hidden_width),
            shape_of(hidden_width, width),
        ),
        [pltpu.VMEM((tok, 3 * width), BF16)] * 2
        + [pltpu.VMEM((width, 3 * tok), BF16)] * 2
        + [pltpu.VMEM((tok, width), F32)],
        10**10,
    )(first, returned, cotangent[0], w_up, w_down)
    grads = []
    for grad in (grad_up, grad_down):
        part = lax.psum_scatter(grad, "scene", scatter_dimension=0, tiled=True)
        grads.append(lax.psum_scatter(part, "batch", scatter_dimension=1, tiled=True))
    return (block_out[None], grad_mid[None], *grads)


def solution(mesh):
    tokens = P("batch", "scene", None)
    return jax.shard_map(
        on_device,
        mesh=mesh,
        in_specs=(tokens, P(None, "batch", "scene"), tokens) + (P(),) * 6,
        out_specs=(tokens, tokens, P("scene", "batch"), P("scene", "batch")),
        check_vma=False,
    )
```

```python
import functools

import jax
import jax.numpy as jnp
import numpy as np
from jax import lax
from jax.experimental import pallas as pl
from jax.experimental.pallas import tpu as pltpu
from jax.sharding import PartitionSpec as P

GROUP = 32
HALO = 64
TILE = 128
F32 = jnp.float32
BF16 = jnp.bfloat16
MESH = pl.DeviceIdType.MESH
VMEM_LIMIT = 56 * 1024 * 1024


def split(x):
    hi = x.astype(BF16)
    return hi, (x - hi.astype(F32)).astype(BF16)


def left3(x, axis=1):
    hi, lo = split(x)
    return jnp.concatenate([hi, hi, lo], axis=axis)


def right3(x, axis=0):
    hi, lo = split(x)
    return jnp.concatenate([hi, lo, hi], axis=axis)


def dot(a, b):
    return lax.dot_general(a, b, (((1,), (0,)), ((), ())), preferred_element_type=F32)


def dot_t(a, b):
    return lax.dot_general(a, b, (((1,), (1,)), ((), ())), preferred_element_type=F32)


def norm_of(values):
    average = jnp.mean(values, axis=-1, keepdims=True)
    centered = values - average
    variance = jnp.mean(centered * centered, axis=-1, keepdims=True)
    scale = lax.rsqrt(variance + 1e-05)
    return centered * scale, scale


def conv_kernel(local_ref, low_ref, high_ref, offset_ref, weight_ref, first_ref, normed_ref, ext, off_t):
    tok, width = local_ref.shape
    taps = weight_ref.shape[0]
    for start, ref in ((0, low_ref), (HALO, local_ref), (HALO + tok, high_ref)):
        hi, lo = split(ref[...])
        ext[pl.ds(start, ref.shape[0]), :width] = hi
        ext[pl.ds(start, ref.shape[0]), width:] = lo
    for b in range(tok // TILE):
        piece = offset_ref[:, b * TILE : (b + 1) * TILE]
        piece = jnp.where(piece > HALO, 4 * TILE, piece).astype(F32)
        piece = jnp.concatenate([piece, jnp.zeros((TILE - taps, TILE), F32)], axis=0)
        off_t[b * TILE : (b + 1) * TILE, :] = piece.T
    span = TILE + 2 * HALO
    base = (
        lax.broadcasted_iota(jnp.int32, (TILE, span), 1)
        - lax.broadcasted_iota(jnp.int32, (TILE, span), 0)
        - HALO
    ).astype(F32)

    @pl.loop(0, tok // TILE)
    def _(b):
        row = pl.multiple_of(b * TILE, TILE)
        window = ext[pl.ds(row, span), :]
        offsets = off_t[pl.ds(row, TILE), :]
        total = local_ref[pl.ds(row, TILE), :]
        for a in range(taps):
            pick = jnp.where(base == offsets[:, a : a + 1], 1.0, 0.0).astype(BF16)
            found = dot(pick, window)
            total += (found[:, :width] + found[:, width:]) * weight_ref[a : a + 1, :]
        first_ref[pl.ds(row, TILE), :] = total
        normed_ref[pl.ds(row, TILE), :] = norm_of(total)[0]


def attend_kernel(head_dim, x_ref, perm_ref, back_ref, wqkv_ref, wout_ref, bias_ref, out_ref, qkv, att):
    tok, width = x_ref.shape
    hi, lo = split(x_ref[...])
    hi = dot(perm_ref[...], hi).astype(BF16)
    lo = dot(perm_ref[...], lo).astype(BF16)
    rows3 = jnp.concatenate([hi, hi, lo], axis=1)
    for part in range(3):
        qkv[:, part * width : (part + 1) * width] = dot(
            rows3, right3(wqkv_ref[:, part * width : (part + 1) * width])
        )
    per_lane = TILE // head_dim
    shape = (TILE, TILE)
    same = (lax.broadcasted_iota(jnp.int32, shape, 0) ^ lax.broadcasted_iota(jnp.int32, shape, 1)) < GROUP
    away = jnp.where(same, 0.0, -1e30)
    lane = lax.broadcasted_iota(jnp.int32, shape, 1)

    @pl.loop(0, tok // TILE)
    def _(b):
        row = pl.ds(pl.multiple_of(b * TILE, TILE), TILE)
        for part in range(width // TILE):
            at = part * TILE
            q = qkv[row, at : at + TILE] * (head_dim**-0.5)
            k = qkv[row, width + at : width + at + TILE]
            v = qkv[row, 2 * width + at : 2 * width + at + TILE]
            keys, values = [], []
            for h in range(per_lane):
                mine = (lane >= h * head_dim) & (lane < (h + 1) * head_dim)
                keys.append(right3(jnp.where(mine, k, 0.0), axis=1))
                values.append(jnp.concatenate(split(jnp.where(mine, v, 0.0)), axis=1))
            scores = dot_t(left3(q), jnp.concatenate(keys, axis=0))
            his, los = [], []
            for h in range(per_lane):
                bias = jnp.concatenate([bias_ref[part * per_lane + h]] * (TILE // GROUP), axis=0)
                s = scores[:, h * TILE : (h + 1) * TILE] + bias + away
                e = jnp.exp(s - jnp.max(s, axis=-1, keepdims=True))
                p = e / jnp.sum(e, axis=-1, keepdims=True)
                p_hi, p_lo = split(p)
                his.append(p_hi)
                los.append(p_lo)
            values = jnp.concatenate(values, axis=0)
            both = dot(jnp.concatenate(his, axis=1), values)
            rest = dot(jnp.concatenate(los, axis=1), values[:, :TILE])
            att[row, at : at + TILE] = both[:, :TILE] + both[:, TILE:] + rest

    hi, lo = split(att[...])
    hi = dot(back_ref[...], hi).astype(BF16)
    lo = dot(back_ref[...], lo).astype(BF16)
    out_ref[...] = dot(jnp.concatenate([hi, hi, lo], axis=1), right3(wout_ref[...]))


def mlp_kernel(
    grad_scale, first_ref, mixed_ref, cot_ref, up_ref, down_ref,
    out_ref, mid_ref, gup_ref, gdown_ref,
    n_left, c_left, nt_left, ct_left, grad_normed,
):
    tok, width = first_ref.shape
    hidden_width = up_ref.shape[1]
    chunk = 2 * TILE
    middle = first_ref[...] + mixed_ref[...]
    normed, scale = norm_of(middle)
    cot = cot_ref[...]
    n_left[...] = left3(normed)
    c_left[...] = left3(cot)
    nt_left[...] = left3(normed.T * grad_scale)
    ct_left[...] = left3(cot.T * grad_scale)
    out_ref[...] = middle
    grad_normed[...] = jnp.zeros_like(grad_normed)

    @pl.loop(0, hidden_width // chunk)
    def _(c):
        at = pl.ds(pl.multiple_of(c * chunk, chunk), chunk)
        up_hi, up_lo = split(up_ref[:, at])
        down_hi, down_lo = split(down_ref[at, :])
        hidden = dot(n_left[...], jnp.concatenate([up_hi, up_lo, up_hi], axis=0))
        grad_act = dot_t(c_left[...], jnp.concatenate([down_hi, down_lo, down_hi], axis=1))
        cdf = 0.5 * (1.0 + lax.erf(hidden * (0.5**0.5)))
        act = hidden * cdf
        density = jnp.exp(-0.5 * hidden * hidden) * ((2.0 * np.pi) ** -0.5)
        grad_hidden = grad_act * (cdf + hidden * density)
        act_hi, act_lo = split(act)
        gh_hi, gh_lo = split(grad_hidden)
        gup_ref[:, at] = dot(nt_left[...], jnp.concatenate([gh_hi, gh_lo, gh_hi], axis=0))
        gdown_ref[at, :] = dot(ct_left[...], jnp.concatenate([act_hi, act_lo, act_hi], axis=0)).T
        out_ref[...] += dot(
            jnp.concatenate([act_hi, act_hi, act_lo], axis=1),
            jnp.concatenate([down_hi, down_lo, down_hi], axis=0),
        )
        grad_normed[...] += dot_t(
            jnp.concatenate([gh_hi, gh_hi, gh_lo], axis=1),
            jnp.concatenate([up_hi, up_lo, up_hi], axis=1),
        )

    g = grad_normed[...]
    along = jnp.mean(g * normed, axis=-1, keepdims=True)
    mid_ref[...] = cot + scale * (g - jnp.mean(g, axis=-1, keepdims=True) - normed * along)


def bits_of(index, order):
    return tuple((index >> bit) & 1 for bit in order)


def block_kernel(
    grad_scale, orders_ab, batch_count, head_dim,
    local_ref, offset_ref, weight_ref, up_hbm, down_hbm, qkv_hbm, wout_hbm, cot_hbm, bias_ref,
    spread_ref, gather_ref, slots_ref, unslots_ref,
    out_ref, mid_ref, gup_ref, gdown_ref,
    up_ref, down_ref, wqkv_ref, wout_ref, cot_ref, load_sem,
    low, high, halo_send, halo_recv, ext, off_t, first_ref,
    x_send, x_recv, y_send, y_recv, xs_sem, xr_sem, ys_sem, yr_sem,
    wqkv3, wout3, bias_tile, up_hi, up_lo, down_hi, down_lo,
    n_left, c_left, nt_left, ct_left, slope, act_hi, act_lo, gh_hi, gh_lo,
    acc_a, acc_b, recv_a, recv_b, zrecv_a, zsend_b, zrecv_b,
    send_sem, recv_sem, za_send, za_recv, zb_send, zb_recv,
):
    tok, width = local_ref.shape
    hidden_width = up_ref.shape[1]
    steps = len(orders_ab[0])
    scene_count = 2**steps
    rows_a, rows_b = width // scene_count, hidden_width // scene_count
    cols_a, cols_b = hidden_width // batch_count, width // batch_count
    pieces_a, pieces_b = cols_a // TILE, width // TILE
    tiles = tok // TILE
    me, my_batch = lax.axis_index("scene"), lax.axis_index("batch")
    values = [(me // 2**bit) % 2 for bit in range(steps)]
    partners = [me + (1 - 2 * values[bit]) * 2**bit for bit in range(steps)]
    others = [lax.rem(my_batch + d, batch_count) for d in range(1, batch_count)]
    scenes = [lax.rem(me + d, scene_count) for d in range(1, scene_count)]

    barrier = pltpu.get_barrier_semaphore()
    for other in scenes:
        pl.semaphore_signal(barrier, inc=1, device_id={"scene": other}, device_id_type=MESH)
    for other in others:
        pl.semaphore_signal(barrier, inc=1, device_id={"batch": other}, device_id_type=MESH)
    loads = [
        pltpu.make_async_copy(source, target, load_sem.at[i])
        for i, (source, target) in enumerate(
            (
                (qkv_hbm, wqkv_ref),
                (wout_hbm, wout_ref),
                (cot_hbm, cot_ref),
                (up_hbm, up_ref),
                (down_hbm, down_ref),
            )
        )
    ]
    for load in loads:
        load.start()

    sent = []

    def start(copy):
        copy.start()
        sent.append(copy)

    def to_scene(source, target, send, recv, other):
        return pltpu.make_async_remote_copy(
            src_ref=source,
            dst_ref=target,
            send_sem=send,
            recv_sem=recv,
            device_id={"scene": other},
            device_id_type=MESH,
        )

    halo = [
        to_scene(local_ref.at[pl.ds(tok - HALO, HALO)], low, halo_send.at[0], halo_recv.at[0], scenes[0]),
        to_scene(local_ref.at[pl.ds(0, HALO)], high, halo_send.at[1], halo_recv.at[1], scenes[-1]),
    ]
    pl.semaphore_wait(barrier, scene_count + batch_count - 2)
    for copy in halo:
        start(copy)

    taps = weight_ref.shape[0]
    span = TILE + 2 * HALO

    def extend(row, block):
        hi, lo = split(block)
        ext[pl.ds(row, block.shape[0]), :width] = hi
        ext[pl.ds(row, block.shape[0]), width:] = lo

    extend(HALO, local_ref[...])
    for t in range(tiles):
        piece = offset_ref[:, t * TILE : (t + 1) * TILE]
        piece = jnp.where(piece > HALO, 4 * TILE, piece).astype(F32)
        piece = jnp.concatenate([piece, jnp.zeros((TILE - taps, TILE), F32)], axis=0)
        off_t[t * TILE : (t + 1) * TILE, :] = piece.T
    base = (
        lax.broadcasted_iota(jnp.int32, (TILE, span), 1)
        - lax.broadcasted_iota(jnp.int32, (TILE, span), 0)
        - HALO
    ).astype(F32)

    def convolve(t):
        row = pl.multiple_of(t * TILE, TILE)
        window = ext[pl.ds(row, span), :]
        offsets = off_t[pl.ds(row, TILE), :]
        total = local_ref[pl.ds(row, TILE), :]
        for a in range(taps):
            pick = jnp.where(base == offsets[:, a : a + 1], 1.0, 0.0).astype(BF16)
            found = dot(pick, window)
            total += (found[:, :width] + found[:, width:]) * weight_ref[a : a + 1, :]
        first_ref[pl.ds(row, TILE), :] = total

    pl.loop(1, tiles - 1)(convolve)
    for copy in halo:
        copy.wait_recv()
    extend(0, jnp.where(me == 0, 0.0, low[...]))
    extend(HALO + tok, jnp.where(me == scene_count - 1, 0.0, high[...]))
    pl.loop(0, 2)(lambda j: convolve(j * (tiles - 1)))

    def move(matrix, rows):
        hi, lo = split(rows)
        return dot(matrix, hi), dot(matrix, lo)

    piece_rows = TILE // scene_count
    hi, lo = move(spread_ref[...], norm_of(first_ref[...])[0])
    x_send[...] = (hi + lo).reshape(x_send.shape)

    def exchange(source, target, t, d, send, recv):
        return to_scene(
            source.at[t, scenes[d]], target.at[t, me], send.at[t, d], recv.at[t, d], scenes[d]
        )

    for t in range(tiles):
        for d in range(scene_count - 1):
            start(exchange(x_send, x_recv, t, d, xs_sem, xr_sem))
        x_recv[t, me] = x_send[t, me]

    loads[0].wait()
    for part in range(3):
        at = slice(part * width, (part + 1) * width)
        wqkv3[:, at] = right3(wqkv_ref[:, at])
    loads[1].wait()
    wout3[...] = right3(wout_ref[...])
    for h in range(bias_ref.shape[0]):
        bias_tile[h] = jnp.concatenate([bias_ref[h]] * (TILE // GROUP), axis=1)
    shape = (TILE, TILE)
    same = (lax.broadcasted_iota(jnp.int32, shape, 0) ^ lax.broadcasted_iota(jnp.int32, shape, 1)) < GROUP
    away = jnp.where(same, 0.0, -1e30)
    lane = lax.broadcasted_iota(jnp.int32, shape, 1)
    per_lane = TILE // head_dim

    def attend(qkv, part):
        at = part * TILE
        q = qkv[:, at : at + TILE] * (head_dim**-0.5)
        k = qkv[:, width + at : width + at + TILE]
        v = qkv[:, 2 * width + at : 2 * width + at + TILE]
        keys, vals = [], []
        for h in range(per_lane):
            mine = (lane >= h * head_dim) & (lane < (h + 1) * head_dim)
            keys.append(right3(jnp.where(mine, k, 0.0), axis=1))
            vals.append(jnp.concatenate(split(jnp.where(mine, v, 0.0)), axis=1))
        scores = dot_t(left3(q), jnp.concatenate(keys, axis=0))
        his, los = [], []
        for h in range(per_lane):
            bias = jnp.concatenate([bias_tile[part * per_lane + h]] * (TILE // GROUP), axis=0)
            s = scores[:, h * TILE : (h + 1) * TILE] + bias + away
            e = jnp.exp(s - jnp.max(s, axis=-1, keepdims=True))
            p_hi, p_lo = split(e / jnp.sum(e, axis=-1, keepdims=True))
            his.append(p_hi)
            los.append(p_lo)
        vals = jnp.concatenate(vals, axis=0)
        both = dot(jnp.concatenate(his, axis=1), vals)
        rest = dot(jnp.concatenate(los, axis=1), vals[:, :TILE])
        return both[:, :TILE] + both[:, TILE:] + rest

    for t in range(tiles):
        for d in range(scene_count - 1):
            exchange(x_send, x_recv, t, d, xs_sem, xr_sem).wait_recv()
        hi, lo = move(slots_ref[...], x_recv[t].reshape(TILE, width))
        hi, lo = hi.astype(BF16), lo.astype(BF16)
        qkv = dot(jnp.concatenate([hi, hi, lo], axis=1), wqkv3[...])
        att = jnp.concatenate([attend(qkv, part) for part in range(width // TILE)], axis=1)
        hi, lo = move(unslots_ref[...], att)
        hi, lo = hi.astype(BF16), lo.astype(BF16)
        mixed = dot(jnp.concatenate([hi, hi, lo], axis=1), wout3[...])
        y_send[t] = mixed.reshape(scene_count, piece_rows, width)
        for d in range(scene_count - 1):
            start(exchange(y_send, y_recv, t, d, ys_sem, yr_sem))
        y_recv[t, me] = y_send[t, me]

    loads[2].wait()
    cot = cot_ref[...]
    c_left[...] = left3(cot)
    cot_t = cot.T * grad_scale
    sub = TILE // batch_count
    ct_left[...] = left3(
        jnp.concatenate(
            [
                cot_t[b * cols_b + q * sub : b * cols_b + (q + 1) * sub]
                for q in range(pieces_b)
                for b in range(batch_count)
            ],
            axis=0,
        )
    )
    for load, source, hi_ref, lo_ref in ((loads[3], up_ref, up_hi, up_lo), (loads[4], down_ref, down_hi, down_lo)):
        load.wait()
        hi, lo = split(source[...])
        hi_ref[...] = hi
        lo_ref[...] = lo

    accs, recvs = (acc_a, acc_b), (recv_a, recv_b)

    def kept(stream, upto):
        return tuple(values[bit] for bit in orders_ab[stream][:upto])

    def halving(stream, q, i):
        bit = orders_ab[stream][i]
        return to_scene(
            accs[stream].at[(q, *kept(stream, i), 1 - values[bit])],
            recvs[stream][i].at[q],
            send_sem.at[stream, q, i],
            recv_sem.at[stream, q, i],
            partners[bit],
        )

    def to_batch(stream, q, d):
        send, recv = ((za_send, za_recv), (zb_send, zb_recv))[stream]
        source = acc_a.at[(q, *kept(0, steps), others[d])] if stream == 0 else zsend_b.at[q, others[d]]
        return pltpu.make_async_remote_copy(
            src_ref=source,
            dst_ref=(zrecv_a, zrecv_b)[stream].at[q, d],
            send_sem=send.at[q, d],
            recv_sem=recv.at[q, d],
            device_id={"batch": others[d]},
            device_id_type=MESH,
        )

    def advance(stream, q, i):
        halving(stream, q, i).wait_recv()
        mine = (q, *kept(stream, i + 1))
        accs[stream][mine] = accs[stream][mine] + recvs[stream][i][q]
        if i + 1 < steps:
            start(halving(stream, q, i + 1))
            return
        if stream == 1:
            pad = jnp.zeros((zsend_b.shape[-1] - rows_b, TILE), F32)
            whole = jnp.concatenate([acc_b[mine], pad], axis=0)
            zsend_b[q] = whole.T.reshape(zsend_b.shape[1:])
        for d in range(batch_count - 1):
            start(to_batch(stream, q, d))

    for t in range(tiles):
        for d in range(scene_count - 1):
            exchange(y_send, y_recv, t, d, ys_sem, yr_sem).wait_recv()
    hi, lo = move(gather_ref[...], y_recv[...].reshape(tok, width))
    middle = first_ref[...] + (hi + lo)
    normed, scale = norm_of(middle)
    n_left[...] = left3(normed)

    chunk = 2 * rows_b
    for c in range(hidden_width // chunk):
        at = slice(c * chunk, (c + 1) * chunk)
        hidden = dot(n_left[...], jnp.concatenate([up_hi[:, at], up_lo[:, at], up_hi[:, at]], axis=0))
        cdf = 0.5 * (1.0 + lax.erf(hidden * (0.5**0.5)))
        density = jnp.exp(-0.5 * hidden * hidden) * ((2.0 * np.pi) ** -0.5)
        slope[:, at] = cdf + hidden * density
        hi, lo = split(hidden * cdf)
        act_hi[:, at] = hi
        act_lo[:, at] = lo
        grad = dot(ct_left[...], jnp.concatenate([hi, lo, hi], axis=0)).T
        for half in range(2):
            block = bits_of(2 * c + half, orders_ab[1])
            for q in range(pieces_b):
                acc_b[(q, *block)] = grad[half * rows_b : (half + 1) * rows_b, q * TILE : (q + 1) * TILE]
    for q in range(pieces_b):
        start(halving(1, q, 0))
    nt_left[...] = left3(normed.T * grad_scale)

    part = batch_count * TILE
    wheres = [
        [slice(b * cols_a + q * TILE, b * cols_a + (q + 1) * TILE) for b in range(batch_count)]
        for q in range(pieces_a)
    ]
    for q in range(pieces_a):
        d_hi = jnp.concatenate([down_hi[w, :] for w in wheres[q]], axis=0)
        d_lo = jnp.concatenate([down_lo[w, :] for w in wheres[q]], axis=0)
        grad_act = dot_t(c_left[...], jnp.concatenate([d_hi, d_lo, d_hi], axis=1))
        hi, lo = split(grad_act * jnp.concatenate([slope[:, w] for w in wheres[q]], axis=1))
        gh_hi[:, q * part : (q + 1) * part] = hi
        gh_lo[:, q * part : (q + 1) * part] = lo
        grad = dot(nt_left[...], jnp.concatenate([hi, lo, hi], axis=0))
        for s in range(scene_count):
            for b in range(batch_count):
                acc_a[(q, *bits_of(s, orders_ab[0]), b)] = grad[
                    s * rows_a : (s + 1) * rows_a, b * TILE : (b + 1) * TILE
                ]
        start(halving(0, q, 0))
        if q == 0:
            for p in range(pieces_b):
                advance(1, p, 0)
        else:
            advance(0, q - 1, 0)

    out_ref[...] = (
        middle
        + dot(act_hi[...], down_hi[...])
        + dot(act_hi[...], down_lo[...])
        + dot(act_lo[...], down_hi[...])
    )
    advance(0, pieces_a - 1, 0)
    advance(1, 0, 1)
    advance(0, 0, 1)

    g = jnp.zeros((tok, width), F32)
    for q in range(pieces_a):
        u_hi = jnp.concatenate([up_hi[:, w] for w in wheres[q]], axis=1)
        u_lo = jnp.concatenate([up_lo[:, w] for w in wheres[q]], axis=1)
        hi, lo = gh_hi[:, q * part : (q + 1) * part], gh_lo[:, q * part : (q + 1) * part]
        g += dot_t(hi, u_hi) + dot_t(hi, u_lo) + dot_t(lo, u_hi)
    along = jnp.mean(g * normed, axis=-1, keepdims=True)
    mid_ref[...] = cot_ref[...] + scale * (g - jnp.mean(g, axis=-1, keepdims=True) - normed * along)

    for i in range(1, steps):
        for q in range(max(pieces_a, pieces_b)):
            for stream, count in ((1, pieces_b), (0, pieces_a)):
                if q < count and not (i == 1 and q == 0):
                    advance(stream, q, i)
    rows = []
    for q in range(pieces_b):
        total = zsend_b[q, my_batch]
        for d in range(batch_count - 1):
            to_batch(1, q, d).wait_recv()
            total += zrecv_b[q, d]
        rows.append(total)
    rows.append(jnp.zeros((TILE - cols_b, rows[0].shape[1]), F32))
    gdown_ref[...] = jnp.concatenate(rows, axis=0).T[:rows_b, :cols_b]
    for q in range(pieces_a):
        total = acc_a[(q, *kept(0, steps), my_batch)]
        for d in range(batch_count - 1):
            to_batch(0, q, d).wait_recv()
            total += zrecv_a[q, d]
        gup_ref[:, q * TILE : (q + 1) * TILE] = total
    for copy in sent:
        copy.wait_send()


def can_fuse(tok, width, head_dim, taps, hidden_width, scene_count, batch_count):
    return (
        scene_count >= 4
        and scene_count & (scene_count - 1) == 0
        and GROUP % scene_count == 0
        and (TILE // scene_count) % 8 == 0
        and batch_count > 1
        and tok % TILE == 0
        and tok // TILE > 1
        and width % TILE == 0
        and TILE % head_dim == 0
        and taps <= TILE
        and TILE % (8 * batch_count) == 0
        and (width // scene_count) % 8 == 0
        and (hidden_width // scene_count) % 64 == 0
        and (hidden_width // batch_count) % TILE == 0
        and width // batch_count < TILE
    )


def piece_orders(tok, scene_count):
    per, count, some = GROUP // scene_count, tok // GROUP, TILE // GROUP
    row = np.arange(tok)
    tile, rest = row // TILE, row % TILE
    device, k, g = rest // (per * some), rest // some % per, rest % some
    spread = np.zeros((tok, tok), np.float32)
    spread[row, (k * scene_count + device) * count + tile * some + g] = 1.0
    row = np.arange(TILE)
    slots = np.zeros((TILE, TILE), np.float32)
    slots[row, row % GROUP * some + row // GROUP] = 1.0
    return spread, slots


def fused(scene_count, batch_count, local, offsets, cot, conv_weight, w_qkv, w_out, score_bias, w_up, w_down):
    tok, width = local.shape
    hidden_width = w_up.shape[1]
    heads = score_bias.shape[0]
    steps = scene_count.bit_length() - 1
    orders_ab = (tuple(range(steps)), (0, *reversed(range(1, steps))))
    rows_a, rows_b = width // scene_count, hidden_width // scene_count
    cols_a = hidden_width // batch_count
    cols_b = width // batch_count
    pieces_a, pieces_b = cols_a // TILE, width // TILE
    tail_a, tail_b = (batch_count, rows_a, TILE), (rows_b, TILE)
    padded = -(-rows_b // TILE) * TILE
    sub = TILE // batch_count
    tiles = tok // TILE
    sems = pltpu.SemaphoreType.DMA
    scratch = (
        [pltpu.VMEM(x.shape, F32) for x in (w_up, w_down, w_qkv, w_out, cot)]
        + [sems((5,))]
        + [pltpu.VMEM((HALO, width), F32)] * 2
        + [sems((2,))] * 2
        + [
            pltpu.VMEM((tok + 2 * HALO, 2 * width), BF16),
            pltpu.VMEM((tok, TILE), F32),
            pltpu.VMEM((tok, width), F32),
        ]
        + [pltpu.VMEM((tiles, scene_count, TILE // scene_count, width), F32)] * 4
        + [sems((tiles, scene_count - 1))] * 4
        + [
            pltpu.VMEM((3 * width, 3 * width), BF16),
            pltpu.VMEM((3 * width, width), BF16),
            pltpu.VMEM((heads, GROUP, TILE), F32),
        ]
        + [pltpu.VMEM(w_up.shape, BF16)] * 2
        + [pltpu.VMEM(w_down.shape, BF16)] * 2
        + [pltpu.VMEM((tok, 3 * width), BF16)] * 2
        + [pltpu.VMEM((width, 3 * tok), BF16)] * 2
        + [pltpu.VMEM((tok, hidden_width), F32)]
        + [pltpu.VMEM((tok, hidden_width), BF16)] * 4
        + [
            pltpu.VMEM((pieces_a, *(2,) * steps, *tail_a), F32),
            pltpu.VMEM((pieces_b, *(2,) * steps, *tail_b), F32),
            [pltpu.VMEM((pieces_a, *(2,) * (steps - 1 - i), *tail_a), F32) for i in range(steps)],
            [pltpu.VMEM((pieces_b, *(2,) * (steps - 1 - i), *tail_b), F32) for i in range(steps)],
            pltpu.VMEM((pieces_a, batch_count - 1, rows_a, TILE), F32),
            pltpu.VMEM((pieces_b, batch_count, sub, padded), F32),
            pltpu.VMEM((pieces_b, batch_count - 1, sub, padded), F32),
        ]
        + [sems((2, max(pieces_a, pieces_b), steps))] * 2
        + [sems((pieces_a, batch_count - 1))] * 2
        + [sems((pieces_b, batch_count - 1))] * 2
    )
    spread, slots = piece_orders(tok, scene_count)
    moves = [jnp.asarray(x, BF16) for x in (spread, spread.T, slots, slots.T)]
    grad_scale = float(tok * scene_count * batch_count) ** -0.5
    vmem, anywhere = pl.BlockSpec(memory_space=pltpu.VMEM), pl.BlockSpec(memory_space=pl.ANY)
    return pl.pallas_call(
        functools.partial(block_kernel, grad_scale, orders_ab, batch_count, width // heads),
        in_specs=[vmem] * 3 + [anywhere] * 5 + [vmem] * 5,
        out_shape=(
            shape_of(tok, width),
            shape_of(tok, width),
            shape_of(rows_a, cols_a),
            shape_of(rows_b, cols_b),
        ),
        scratch_shapes=scratch,
        compiler_params=pltpu.CompilerParams(
            vmem_limit_bytes=VMEM_LIMIT, collective_id=0, has_side_effects=True
        ),
    )(local, offsets, conv_weight, w_up, w_down, w_qkv, w_out, cot, score_bias, *moves)


def shape_of(*dims):
    return jax.ShapeDtypeStruct(dims, F32)


def call(kernel, outs, scratch, flops):
    return pl.pallas_call(
        kernel,
        out_shape=outs,
        scratch_shapes=scratch,
        compiler_params=pltpu.CompilerParams(vmem_limit_bytes=VMEM_LIMIT),
        cost_estimate=pl.CostEstimate(flops=flops, bytes_accessed=4000000, transcendentals=0),
    )


def orders(tok, scene_count):
    per, count = GROUP // scene_count, tok // GROUP
    row = np.arange(tok)
    group, slot = row // GROUP, row % GROUP
    source = ((slot % per) * scene_count + slot // per) * count + group
    perm = np.zeros((tok, tok), np.float32)
    perm[row, source] = 1.0
    return perm


def on_device(tokens, nbr_offset, cotangent, conv_weight, w_qkv, w_out, score_bias, w_up, w_down):
    local = tokens[0]
    tok, width = local.shape
    hidden_width = w_up.shape[1]
    heads = score_bias.shape[0]
    scene_count = lax.axis_size("scene")
    batch_count = lax.axis_size("batch")
    if can_fuse(
        tok, width, width // heads, conv_weight.shape[0], hidden_width, scene_count, batch_count
    ):
        block_out, grad_mid, *grads = fused(
            scene_count, batch_count, local, nbr_offset[:, 0, :], cotangent[0],
            conv_weight, w_qkv, w_out, score_bias, w_up, w_down,
        )
        return (block_out[None], grad_mid[None], *grads)
    forward = [(i, i + 1) for i in range(scene_count - 1)]
    backward = [(target, source) for source, target in forward]
    low = lax.ppermute(local[tok - HALO :], "scene", forward)
    high = lax.ppermute(local[:HALO], "scene", backward)
    first, normed = call(
        conv_kernel,
        (shape_of(tok, width), shape_of(tok, width)),
        [pltpu.VMEM((tok + 2 * HALO, 2 * width), BF16), pltpu.VMEM((tok, TILE), F32)],
        8 * 10**9,
    )(local, low, high, nbr_offset[:, 0, :], conv_weight)
    per, count = GROUP // scene_count, tok // GROUP
    blocks = normed.reshape(per, scene_count, count, width)
    arrived = lax.all_to_all(blocks, "scene", split_axis=1, concat_axis=1, tiled=True)
    perm = orders(tok, scene_count)
    bias = jnp.tile(score_bias, (1, 1, TILE // GROUP))
    mixed = call(
        functools.partial(attend_kernel, width // heads),
        shape_of(tok, width),
        [pltpu.VMEM((tok, 3 * width), F32), pltpu.VMEM((tok, width), F32)],
        10**10,
    )(
        arrived.reshape(tok, width),
        jnp.asarray(perm, BF16),
        jnp.asarray(perm.T, BF16),
        w_qkv,
        w_out,
        bias,
    )
    returned = lax.all_to_all(
        mixed.reshape(per, scene_count, count, width), "scene", split_axis=1, concat_axis=1, tiled=True
    ).reshape(tok, width)
    grad_scale = float(tok * scene_count * batch_count) ** -0.5
    block_out, grad_mid, grad_up, grad_down = call(
        functools.partial(mlp_kernel, grad_scale),
        (
            shape_of(tok, width),
            shape_of(tok, width),
            shape_of(width, hidden_width),
            shape_of(hidden_width, width),
        ),
        [pltpu.VMEM((tok, 3 * width), BF16)] * 2
        + [pltpu.VMEM((width, 3 * tok), BF16)] * 2
        + [pltpu.VMEM((tok, width), F32)],
        10**10,
    )(first, returned, cotangent[0], w_up, w_down)
    grads = []
    for grad in (grad_up, grad_down):
        part = lax.psum_scatter(grad, "scene", scatter_dimension=0, tiled=True)
        grads.append(lax.psum_scatter(part, "batch", scatter_dimension=1, tiled=True))
    return (block_out[None], grad_mid[None], *grads)


def solution(mesh):
    tokens = P("batch", "scene", None)
    return jax.shard_map(
        on_device,
        mesh=mesh,
        in_specs=(tokens, P(None, "batch", "scene"), tokens) + (P(),) * 6,
        out_specs=(tokens, tokens, P("scene", "batch"), P("scene", "batch")),
        check_vma=False,
    )
```

```python
import functools

import jax
import jax.numpy as jnp
import numpy as np
from jax import lax
from jax.experimental import pallas as pl
from jax.experimental.pallas import tpu as pltpu
from jax.sharding import PartitionSpec as P

GROUP = 32
HALO = 64
TILE = 128
F32 = jnp.float32
BF16 = jnp.bfloat16
MESH = pl.DeviceIdType.MESH
VMEM_LIMIT = 56 * 1024 * 1024


def split(x):
    hi = x.astype(BF16)
    return hi, (x - hi.astype(F32)).astype(BF16)


def left3(x, axis=1):
    hi, lo = split(x)
    return jnp.concatenate([hi, hi, lo], axis=axis)


def right3(x, axis=0):
    hi, lo = split(x)
    return jnp.concatenate([hi, lo, hi], axis=axis)


def dot(a, b):
    return lax.dot_general(a, b, (((1,), (0,)), ((), ())), preferred_element_type=F32)


def dot_t(a, b):
    return lax.dot_general(a, b, (((1,), (1,)), ((), ())), preferred_element_type=F32)


def norm_of(values):
    average = jnp.mean(values, axis=-1, keepdims=True)
    centered = values - average
    variance = jnp.mean(centered * centered, axis=-1, keepdims=True)
    scale = lax.rsqrt(variance + 1e-05)
    return centered * scale, scale


def conv_kernel(local_ref, low_ref, high_ref, offset_ref, weight_ref, first_ref, normed_ref, ext, off_t):
    tok, width = local_ref.shape
    taps = weight_ref.shape[0]
    for start, ref in ((0, low_ref), (HALO, local_ref), (HALO + tok, high_ref)):
        hi, lo = split(ref[...])
        ext[pl.ds(start, ref.shape[0]), :width] = hi
        ext[pl.ds(start, ref.shape[0]), width:] = lo
    for b in range(tok // TILE):
        piece = offset_ref[:, b * TILE : (b + 1) * TILE]
        piece = jnp.where(piece > HALO, 4 * TILE, piece).astype(F32)
        piece = jnp.concatenate([piece, jnp.zeros((TILE - taps, TILE), F32)], axis=0)
        off_t[b * TILE : (b + 1) * TILE, :] = piece.T
    span = TILE + 2 * HALO
    base = (
        lax.broadcasted_iota(jnp.int32, (TILE, span), 1)
        - lax.broadcasted_iota(jnp.int32, (TILE, span), 0)
        - HALO
    ).astype(F32)

    @pl.loop(0, tok // TILE)
    def _(b):
        row = pl.multiple_of(b * TILE, TILE)
        window = ext[pl.ds(row, span), :]
        offsets = off_t[pl.ds(row, TILE), :]
        total = local_ref[pl.ds(row, TILE), :]
        for a in range(taps):
            pick = jnp.where(base == offsets[:, a : a + 1], 1.0, 0.0).astype(BF16)
            found = dot(pick, window)
            total += (found[:, :width] + found[:, width:]) * weight_ref[a : a + 1, :]
        first_ref[pl.ds(row, TILE), :] = total
        normed_ref[pl.ds(row, TILE), :] = norm_of(total)[0]


def attend_kernel(head_dim, x_ref, perm_ref, back_ref, wqkv_ref, wout_ref, bias_ref, out_ref, qkv, att):
    tok, width = x_ref.shape
    hi, lo = split(x_ref[...])
    hi = dot(perm_ref[...], hi).astype(BF16)
    lo = dot(perm_ref[...], lo).astype(BF16)
    rows3 = jnp.concatenate([hi, hi, lo], axis=1)
    for part in range(3):
        qkv[:, part * width : (part + 1) * width] = dot(
            rows3, right3(wqkv_ref[:, part * width : (part + 1) * width])
        )
    per_lane = TILE // head_dim
    shape = (TILE, TILE)
    same = (lax.broadcasted_iota(jnp.int32, shape, 0) ^ lax.broadcasted_iota(jnp.int32, shape, 1)) < GROUP
    away = jnp.where(same, 0.0, -1e30)
    lane = lax.broadcasted_iota(jnp.int32, shape, 1)

    @pl.loop(0, tok // TILE)
    def _(b):
        row = pl.ds(pl.multiple_of(b * TILE, TILE), TILE)
        for part in range(width // TILE):
            at = part * TILE
            q = qkv[row, at : at + TILE] * (head_dim**-0.5)
            k = qkv[row, width + at : width + at + TILE]
            v = qkv[row, 2 * width + at : 2 * width + at + TILE]
            keys, values = [], []
            for h in range(per_lane):
                mine = (lane >= h * head_dim) & (lane < (h + 1) * head_dim)
                keys.append(right3(jnp.where(mine, k, 0.0), axis=1))
                values.append(jnp.concatenate(split(jnp.where(mine, v, 0.0)), axis=1))
            scores = dot_t(left3(q), jnp.concatenate(keys, axis=0))
            his, los = [], []
            for h in range(per_lane):
                bias = jnp.concatenate([bias_ref[part * per_lane + h]] * (TILE // GROUP), axis=0)
                s = scores[:, h * TILE : (h + 1) * TILE] + bias + away
                e = jnp.exp(s - jnp.max(s, axis=-1, keepdims=True))
                p = e / jnp.sum(e, axis=-1, keepdims=True)
                p_hi, p_lo = split(p)
                his.append(p_hi)
                los.append(p_lo)
            values = jnp.concatenate(values, axis=0)
            both = dot(jnp.concatenate(his, axis=1), values)
            rest = dot(jnp.concatenate(los, axis=1), values[:, :TILE])
            att[row, at : at + TILE] = both[:, :TILE] + both[:, TILE:] + rest

    hi, lo = split(att[...])
    hi = dot(back_ref[...], hi).astype(BF16)
    lo = dot(back_ref[...], lo).astype(BF16)
    out_ref[...] = dot(jnp.concatenate([hi, hi, lo], axis=1), right3(wout_ref[...]))


def mlp_kernel(
    grad_scale, first_ref, mixed_ref, cot_ref, up_ref, down_ref,
    out_ref, mid_ref, gup_ref, gdown_ref,
    n_left, c_left, nt_left, ct_left, grad_normed,
):
    tok, width = first_ref.shape
    hidden_width = up_ref.shape[1]
    chunk = 2 * TILE
    middle = first_ref[...] + mixed_ref[...]
    normed, scale = norm_of(middle)
    cot = cot_ref[...]
    n_left[...] = left3(normed)
    c_left[...] = left3(cot)
    nt_left[...] = left3(normed.T * grad_scale)
    ct_left[...] = left3(cot.T * grad_scale)
    out_ref[...] = middle
    grad_normed[...] = jnp.zeros_like(grad_normed)

    @pl.loop(0, hidden_width // chunk)
    def _(c):
        at = pl.ds(pl.multiple_of(c * chunk, chunk), chunk)
        up_hi, up_lo = split(up_ref[:, at])
        down_hi, down_lo = split(down_ref[at, :])
        hidden = dot(n_left[...], jnp.concatenate([up_hi, up_lo, up_hi], axis=0))
        grad_act = dot_t(c_left[...], jnp.concatenate([down_hi, down_lo, down_hi], axis=1))
        cdf = 0.5 * (1.0 + lax.erf(hidden * (0.5**0.5)))
        act = hidden * cdf
        density = jnp.exp(-0.5 * hidden * hidden) * ((2.0 * np.pi) ** -0.5)
        grad_hidden = grad_act * (cdf + hidden * density)
        act_hi, act_lo = split(act)
        gh_hi, gh_lo = split(grad_hidden)
        gup_ref[:, at] = dot(nt_left[...], jnp.concatenate([gh_hi, gh_lo, gh_hi], axis=0))
        gdown_ref[at, :] = dot(ct_left[...], jnp.concatenate([act_hi, act_lo, act_hi], axis=0)).T
        out_ref[...] += dot(
            jnp.concatenate([act_hi, act_hi, act_lo], axis=1),
            jnp.concatenate([down_hi, down_lo, down_hi], axis=0),
        )
        grad_normed[...] += dot_t(
            jnp.concatenate([gh_hi, gh_hi, gh_lo], axis=1),
            jnp.concatenate([up_hi, up_lo, up_hi], axis=1),
        )

    g = grad_normed[...]
    along = jnp.mean(g * normed, axis=-1, keepdims=True)
    mid_ref[...] = cot + scale * (g - jnp.mean(g, axis=-1, keepdims=True) - normed * along)


def bits_of(index, order):
    return tuple((index >> bit) & 1 for bit in order)


def block_kernel(
    grad_scale, orders_ab, batch_count, head_dim,
    local_ref, offset_ref, weight_ref, up_hbm, down_hbm, qkv_hbm, wout_hbm, cot_hbm, bias_ref,
    spread_ref, gather_ref, slots_ref, unslots_ref,
    out_ref, mid_ref, gup_ref, gdown_ref,
    up_ref, down_ref, wqkv_ref, wout_ref, cot_ref, load_sem,
    low, high, halo_send, halo_recv, ext, off_t, first_ref,
    x_send, x_recv, y_send, y_recv, xs_sem, xr_sem, ys_sem, yr_sem,
    wqkv3, wout3, bias_tile, up_hi, up_lo, down_hi, down_lo,
    n_left, c_left, nt_left, ct_left, slope, act_hi, act_lo, gh_hi, gh_lo,
    acc_a, acc_b, recv_a, recv_b, zrecv_a, zsend_b, zrecv_b,
    send_sem, recv_sem, core_send, core_recv, za_send, za_recv, zb_send, zb_recv,
):
    tok, width = local_ref.shape
    hidden_width = up_ref.shape[1]
    steps = len(orders_ab[0])
    scene_count = 2**steps
    rows_a, rows_b = width // scene_count, hidden_width // scene_count
    cols_a, cols_b = hidden_width // batch_count, width // batch_count
    pieces_a, pieces_b = cols_a // TILE, width // TILE
    tiles = tok // TILE
    me, my_batch = lax.axis_index("scene"), lax.axis_index("batch")
    values = [(me // 2**bit) % 2 for bit in range(steps)]
    partners = [me + (1 - 2 * values[bit]) * 2**bit for bit in range(steps)]
    others = [lax.rem(my_batch + d, batch_count) for d in range(1, batch_count)]
    scenes = [lax.rem(me + d, scene_count) for d in range(1, scene_count)]

    barrier = pltpu.get_barrier_semaphore()
    for other in scenes:
        pl.semaphore_signal(barrier, inc=1, device_id={"scene": other}, device_id_type=MESH)
    for other in others:
        pl.semaphore_signal(barrier, inc=1, device_id={"batch": other}, device_id_type=MESH)
    loads = [
        pltpu.make_async_copy(source, target, load_sem.at[i])
        for i, (source, target) in enumerate(
            (
                (qkv_hbm, wqkv_ref),
                (wout_hbm, wout_ref),
                (cot_hbm, cot_ref),
                (up_hbm, up_ref),
                (down_hbm, down_ref),
            )
        )
    ]
    for load in loads:
        load.start()

    sent = []

    def start(copy):
        copy.start()
        sent.append(copy)

    def to_scene(source, target, send, recv, other):
        return pltpu.make_async_remote_copy(
            src_ref=source,
            dst_ref=target,
            send_sem=send,
            recv_sem=recv,
            device_id={"scene": other},
            device_id_type=MESH,
        )

    halo = [
        to_scene(local_ref.at[pl.ds(tok - HALO, HALO)], low, halo_send.at[0], halo_recv.at[0], scenes[0]),
        to_scene(local_ref.at[pl.ds(0, HALO)], high, halo_send.at[1], halo_recv.at[1], scenes[-1]),
    ]
    taps = weight_ref.shape[0]
    span = TILE + 2 * HALO

    def extend(row, block):
        hi, lo = split(block)
        ext[pl.ds(row, block.shape[0]), :width] = hi
        ext[pl.ds(row, block.shape[0]), width:] = lo

    extend(HALO, local_ref[...])
    for t in range(tiles):
        piece = offset_ref[:, 0, t * TILE : (t + 1) * TILE]
        piece = jnp.where(piece > HALO, 4 * TILE, piece).astype(F32)
        piece = jnp.concatenate([piece, jnp.zeros((TILE - taps, TILE), F32)], axis=0)
        off_t[t * TILE : (t + 1) * TILE, :] = piece.T
    for h in range(bias_ref.shape[0]):
        bias_tile[h] = jnp.concatenate([bias_ref[h]] * (TILE // GROUP), axis=1)
    pl.semaphore_wait(barrier, scene_count + batch_count - 2)
    for copy in halo:
        start(copy)
    base = (
        lax.broadcasted_iota(jnp.int32, (TILE, span), 1)
        - lax.broadcasted_iota(jnp.int32, (TILE, span), 0)
        - HALO
    ).astype(F32)

    def convolve(t):
        row = pl.multiple_of(t * TILE, TILE)
        window = ext[pl.ds(row, span), :]
        offsets = off_t[pl.ds(row, TILE), :]
        total = local_ref[pl.ds(row, TILE), :]
        for a in range(taps):
            pick = jnp.where(base == offsets[:, a : a + 1], 1.0, 0.0).astype(BF16)
            found = dot(pick, window)
            total += (found[:, :width] + found[:, width:]) * weight_ref[a : a + 1, :]
        first_ref[pl.ds(row, TILE), :] = total

    pl.loop(1, tiles - 1)(convolve)
    for copy in halo:
        copy.wait_recv()
    extend(0, jnp.where(me == 0, 0.0, low[...]))
    extend(HALO + tok, jnp.where(me == scene_count - 1, 0.0, high[...]))
    pl.loop(0, 2)(lambda j: convolve(j * (tiles - 1)))

    def move(matrix, rows):
        hi, lo = split(rows)
        return dot(matrix, hi), dot(matrix, lo)

    piece_rows = TILE // scene_count
    hi, lo = move(spread_ref[...], norm_of(first_ref[...])[0])
    x_send[...] = (hi + lo).reshape(x_send.shape)

    def exchange(source, target, t, d, send, recv):
        return to_scene(
            source.at[t, scenes[d]], target.at[t, me], send.at[t, d], recv.at[t, d], scenes[d]
        )

    for t in range(tiles):
        for d in range(scene_count - 1):
            start(exchange(x_send, x_recv, t, d, xs_sem, xr_sem))
        x_recv[t, me] = x_send[t, me]

    loads[0].wait()
    for part in range(3):
        at = slice(part * width, (part + 1) * width)
        wqkv3[:, at] = right3(wqkv_ref[:, at])
    loads[1].wait()
    wout3[...] = right3(wout_ref[...])
    shape = (TILE, TILE)
    same = (lax.broadcasted_iota(jnp.int32, shape, 0) ^ lax.broadcasted_iota(jnp.int32, shape, 1)) < GROUP
    away = jnp.where(same, 0.0, -1e30)
    lane = lax.broadcasted_iota(jnp.int32, shape, 1)
    per_lane = TILE // head_dim

    def attend(qkv, part):
        at = part * TILE
        q = qkv[:, at : at + TILE] * (head_dim**-0.5)
        k = qkv[:, width + at : width + at + TILE]
        v = qkv[:, 2 * width + at : 2 * width + at + TILE]
        keys, vals = [], []
        for h in range(per_lane):
            mine = (lane >= h * head_dim) & (lane < (h + 1) * head_dim)
            keys.append(right3(jnp.where(mine, k, 0.0), axis=1))
            vals.append(jnp.concatenate(split(jnp.where(mine, v, 0.0)), axis=1))
        scores = dot_t(left3(q), jnp.concatenate(keys, axis=0))
        his, los = [], []
        for h in range(per_lane):
            bias = jnp.concatenate([bias_tile[part * per_lane + h]] * (TILE // GROUP), axis=0)
            s = scores[:, h * TILE : (h + 1) * TILE] + bias + away
            e = jnp.exp(s - jnp.max(s, axis=-1, keepdims=True))
            p_hi, p_lo = split(e / jnp.sum(e, axis=-1, keepdims=True))
            his.append(p_hi)
            los.append(p_lo)
        vals = jnp.concatenate(vals, axis=0)
        both = dot(jnp.concatenate(his, axis=1), vals)
        rest = dot(jnp.concatenate(los, axis=1), vals[:, :TILE])
        return both[:, :TILE] + both[:, TILE:] + rest

    for t in range(tiles):
        for d in range(scene_count - 1):
            exchange(x_send, x_recv, t, d, xs_sem, xr_sem).wait_recv()
        hi, lo = move(slots_ref[...], x_recv[t].reshape(TILE, width))
        hi, lo = hi.astype(BF16), lo.astype(BF16)
        qkv = dot(jnp.concatenate([hi, hi, lo], axis=1), wqkv3[...])
        att = jnp.concatenate([attend(qkv, part) for part in range(width // TILE)], axis=1)
        hi, lo = move(unslots_ref[...], att)
        hi, lo = hi.astype(BF16), lo.astype(BF16)
        mixed = dot(jnp.concatenate([hi, hi, lo], axis=1), wout3[...])
        y_send[t] = mixed.reshape(scene_count, piece_rows, width)
        for d in range(scene_count - 1):
            start(exchange(y_send, y_recv, t, d, ys_sem, yr_sem))
        y_recv[t, me] = y_send[t, me]

    loads[2].wait()
    cot = cot_ref[...]
    c_left[...] = left3(cot)
    cot_t = cot.T * grad_scale
    sub = TILE // batch_count
    ct_left[...] = left3(
        jnp.concatenate(
            [
                cot_t[b * cols_b + q * sub : b * cols_b + (q + 1) * sub]
                for q in range(pieces_b)
                for b in range(batch_count)
            ],
            axis=0,
        )
    )
    for load, source, hi_ref, lo_ref in ((loads[3], up_ref, up_hi, up_lo), (loads[4], down_ref, down_hi, down_lo)):
        load.wait()
        hi, lo = split(source[...])
        hi_ref[...] = hi
        lo_ref[...] = lo

    accs, recvs = (acc_a, acc_b), (recv_a, recv_b)

    def kept(stream, upto):
        return tuple(values[bit] for bit in orders_ab[stream][:upto])

    def halving(stream, q, i):
        bit = orders_ab[stream][i]
        return to_scene(
            accs[stream].at[(q, *kept(stream, i), 1 - values[bit])],
            recvs[stream][i].at[q],
            send_sem.at[stream, q, i],
            recv_sem.at[stream, q, i],
            partners[bit],
        )

    def to_batch(stream, q, d):
        send, recv = ((za_send, za_recv), (zb_send, zb_recv))[stream]
        source = acc_a.at[(q, *kept(0, steps), others[d])] if stream == 0 else zsend_b.at[q, others[d]]
        return pltpu.make_async_remote_copy(
            src_ref=source,
            dst_ref=(zrecv_a, zrecv_b)[stream].at[q, d],
            send_sem=send.at[q, d],
            recv_sem=recv.at[q, d],
            device_id={"batch": others[d]},
            device_id_type=MESH,
        )

    done = set()

    def advance(stream, q, i):
        if (stream, q, i) in done:
            return
        done.add((stream, q, i))
        halving(stream, q, i).wait_recv()
        mine = (q, *kept(stream, i + 1))
        accs[stream][mine] = accs[stream][mine] + recvs[stream][i][q]
        if i + 1 < steps:
            start(halving(stream, q, i + 1))
            return
        if stream == 1:
            pad = jnp.zeros((zsend_b.shape[-1] - rows_b, TILE), F32)
            whole = jnp.concatenate([acc_b[mine], pad], axis=0)
            zsend_b[q] = whole.T.reshape(zsend_b.shape[1:])
        for d in range(batch_count - 1):
            start(to_batch(stream, q, d))

    for t in range(tiles):
        for d in range(scene_count - 1):
            exchange(y_send, y_recv, t, d, ys_sem, yr_sem).wait_recv()
    hi, lo = move(gather_ref[...], y_recv[...].reshape(tok, width))
    middle = first_ref[...] + (hi + lo)
    normed, scale = norm_of(middle)
    n_left[...] = left3(normed)

    chunk = 2 * rows_b
    chunks = hidden_width // chunk
    top = values[steps - 1]

    def chunk_at(j):
        return lax.rem((1 - top) * (chunks // 2) + j, chunks)

    def chunk_bits(j):
        return tuple((chunk_at(j) // 2 ** (bit - 1)) % 2 for bit in orders_ab[1][1:])

    def early(q, j):
        return to_scene(
            acc_b.at[(q, 1 - values[0], *chunk_bits(j))],
            recv_b[0].at[(q, *chunk_bits(j))],
            core_send.at[q, j],
            core_recv.at[q, j],
            partners[0],
        )

    def add_early(q, half):
        for j in range(half * (chunks // 2), (half + 1) * (chunks // 2)):
            early(q, j).wait_recv()
        which = (1 - top, top)[half]
        acc_b[q, values[0], which] = acc_b[q, values[0], which] + recv_b[0][q, which]
        if half == 0:
            start(halving(1, q, 1))

    for j in range(chunks):
        at = pl.ds(pl.multiple_of(chunk_at(j) * chunk, chunk), chunk)
        hidden = dot(n_left[...], jnp.concatenate([up_hi[:, at], up_lo[:, at], up_hi[:, at]], axis=0))
        cdf = 0.5 * (1.0 + lax.erf(hidden * (0.5**0.5)))
        density = jnp.exp(-0.5 * hidden * hidden) * ((2.0 * np.pi) ** -0.5)
        slope[:, at] = cdf + hidden * density
        hi, lo = split(hidden * cdf)
        act_hi[:, at] = hi
        act_lo[:, at] = lo
        grad = dot(ct_left[...], jnp.concatenate([hi, lo, hi], axis=0)).T
        for half in range(2):
            for q in range(pieces_b):
                acc_b[(q, half, *chunk_bits(j))] = grad[
                    half * rows_b : (half + 1) * rows_b, q * TILE : (q + 1) * TILE
                ]
        for q in range(pieces_b):
            start(early(q, j))
        if j >= chunks // 2 and j - chunks // 2 < pieces_b:
            add_early(j - chunks // 2, 0)
    nt_left[...] = left3(normed.T * grad_scale)

    part = batch_count * TILE
    wheres = [
        [slice(b * cols_a + q * TILE, b * cols_a + (q + 1) * TILE) for b in range(batch_count)]
        for q in range(pieces_a)
    ]
    for q in range(pieces_a):
        d_hi = jnp.concatenate([down_hi[w, :] for w in wheres[q]], axis=0)
        d_lo = jnp.concatenate([down_lo[w, :] for w in wheres[q]], axis=0)
        grad_act = dot_t(c_left[...], jnp.concatenate([d_hi, d_lo, d_hi], axis=1))
        hi, lo = split(grad_act * jnp.concatenate([slope[:, w] for w in wheres[q]], axis=1))
        gh_hi[:, q * part : (q + 1) * part] = hi
        gh_lo[:, q * part : (q + 1) * part] = lo
        grad = dot(nt_left[...], jnp.concatenate([hi, lo, hi], axis=0))
        for s in range(scene_count):
            for b in range(batch_count):
                acc_a[(q, *bits_of(s, orders_ab[0]), b)] = grad[
                    s * rows_a : (s + 1) * rows_a, b * TILE : (b + 1) * TILE
                ]
        start(halving(0, q, 0))
        if q == 0:
            for p in range(min(chunks // 2 + chunks % 2, pieces_b), pieces_b):
                add_early(p, 0)
            for p in range(pieces_b):
                add_early(p, 1)
        else:
            advance(0, q - 1, 0)
        if q == 1:
            advance(1, 0, 1)

    out_ref[...] = (
        middle
        + dot(act_hi[...], down_hi[...])
        + dot(act_hi[...], down_lo[...])
        + dot(act_lo[...], down_hi[...])
    )
    advance(0, pieces_a - 1, 0)
    for p in range(pieces_b - 1):
        advance(1, p, 1)
    advance(0, 0, 1)

    g = jnp.zeros((tok, width), F32)
    for q in range(pieces_a):
        u_hi = jnp.concatenate([up_hi[:, w] for w in wheres[q]], axis=1)
        u_lo = jnp.concatenate([up_lo[:, w] for w in wheres[q]], axis=1)
        hi, lo = gh_hi[:, q * part : (q + 1) * part], gh_lo[:, q * part : (q + 1) * part]
        g += dot_t(hi, u_hi) + dot_t(hi, u_lo) + dot_t(lo, u_hi)
    along = jnp.mean(g * normed, axis=-1, keepdims=True)
    mid_ref[...] = cot_ref[...] + scale * (g - jnp.mean(g, axis=-1, keepdims=True) - normed * along)

    advance(1, pieces_b - 1, 1)
    if pieces_a > 2:
        advance(0, 1, 1)
    for i in range(1, steps):
        for q in range(max(pieces_a, pieces_b)):
            for stream, count in ((1, pieces_b), (0, pieces_a)):
                if q < count:
                    advance(stream, q, i)
    rows = []
    for q in range(pieces_b):
        total = zsend_b[q, my_batch]
        for d in range(batch_count - 1):
            to_batch(1, q, d).wait_recv()
            total += zrecv_b[q, d]
        rows.append(total)
    rows.append(jnp.zeros((TILE - cols_b, rows[0].shape[1]), F32))
    gdown_ref[...] = jnp.concatenate(rows, axis=0).T[:rows_b, :cols_b]
    for q in range(pieces_a):
        total = acc_a[(q, *kept(0, steps), my_batch)]
        for d in range(batch_count - 1):
            to_batch(0, q, d).wait_recv()
            total += zrecv_a[q, d]
        gup_ref[:, q * TILE : (q + 1) * TILE] = total
    for copy in sent:
        copy.wait_send()


def can_fuse(tok, width, head_dim, taps, hidden_width, scene_count, batch_count):
    return (
        scene_count >= 4
        and scene_count & (scene_count - 1) == 0
        and GROUP % scene_count == 0
        and (TILE // scene_count) % 8 == 0
        and batch_count > 1
        and tok % TILE == 0
        and tok // TILE > 1
        and width % TILE == 0
        and TILE % head_dim == 0
        and taps <= TILE
        and TILE % (8 * batch_count) == 0
        and (width // scene_count) % 8 == 0
        and (hidden_width // scene_count) % 64 == 0
        and (hidden_width // batch_count) % TILE == 0
        and width // batch_count < TILE
    )


def piece_orders(tok, scene_count):
    per, count, some = GROUP // scene_count, tok // GROUP, TILE // GROUP
    row = np.arange(tok)
    tile, rest = row // TILE, row % TILE
    device, k, g = rest // (per * some), rest // some % per, rest % some
    spread = np.zeros((tok, tok), np.float32)
    spread[row, (k * scene_count + device) * count + tile * some + g] = 1.0
    row = np.arange(TILE)
    slots = np.zeros((TILE, TILE), np.float32)
    slots[row, row % GROUP * some + row // GROUP] = 1.0
    return spread, slots


def pieces_of(ref, count):
    rows = ref.shape[0] // count
    return [ref.at[pl.ds(i * rows, rows)] for i in range(count)]


def hand_over_kernel(*refs):
    sources, targets, sem = refs[:4], refs[4:8], refs[8]
    copies = []
    for source, target in zip(sources, targets):
        count = 4 if source.shape[0] % 32 == 0 and source.shape[0] >= 256 else 1
        for a, b in zip(pieces_of(source, count), pieces_of(target, count)):
            copies.append(pltpu.make_async_copy(a, b, sem.at[len(copies)]))
    for copy in copies:
        copy.start()
    for copy in copies:
        copy.wait()


def hand_over(results):
    anywhere = pl.BlockSpec(memory_space=pl.ANY)
    return pl.pallas_call(
        hand_over_kernel,
        in_specs=[anywhere] * 4,
        out_specs=[anywhere] * 4,
        out_shape=tuple(shape_of(*x.shape) for x in results),
        scratch_shapes=[pltpu.SemaphoreType.DMA((16,))],
        compiler_params=pltpu.CompilerParams(vmem_limit_bytes=VMEM_LIMIT),
    )(*results)


def fused(scene_count, batch_count, local, offsets, cot, conv_weight, w_qkv, w_out, score_bias, w_up, w_down):
    tok, width = local.shape
    hidden_width = w_up.shape[1]
    heads = score_bias.shape[0]
    steps = scene_count.bit_length() - 1
    orders_ab = (tuple(range(steps)), (0, *reversed(range(1, steps))))
    rows_a, rows_b = width // scene_count, hidden_width // scene_count
    cols_a = hidden_width // batch_count
    cols_b = width // batch_count
    pieces_a, pieces_b = cols_a // TILE, width // TILE
    tail_a, tail_b = (batch_count, rows_a, TILE), (rows_b, TILE)
    padded = -(-rows_b // TILE) * TILE
    sub = TILE // batch_count
    tiles = tok // TILE
    sems = pltpu.SemaphoreType.DMA
    scratch = (
        [pltpu.VMEM(x.shape, F32) for x in (w_up, w_down, w_qkv, w_out, cot)]
        + [sems((5,))]
        + [pltpu.VMEM((HALO, width), F32)] * 2
        + [sems((2,))] * 2
        + [
            pltpu.VMEM((tok + 2 * HALO, 2 * width), BF16),
            pltpu.VMEM((tok, TILE), F32),
            pltpu.VMEM((tok, width), F32),
        ]
        + [pltpu.VMEM((tiles, scene_count, TILE // scene_count, width), F32)] * 4
        + [sems((tiles, scene_count - 1))] * 4
        + [
            pltpu.VMEM((3 * width, 3 * width), BF16),
            pltpu.VMEM((3 * width, width), BF16),
            pltpu.VMEM((heads, GROUP, TILE), F32),
        ]
        + [pltpu.VMEM(w_up.shape, BF16)] * 2
        + [pltpu.VMEM(w_down.shape, BF16)] * 2
        + [pltpu.VMEM((tok, 3 * width), BF16)] * 2
        + [pltpu.VMEM((width, 3 * tok), BF16)] * 2
        + [pltpu.VMEM((tok, hidden_width), F32)]
        + [pltpu.VMEM((tok, hidden_width), BF16)] * 4
        + [
            pltpu.VMEM((pieces_a, *(2,) * steps, *tail_a), F32),
            pltpu.VMEM((pieces_b, *(2,) * steps, *tail_b), F32),
            [pltpu.VMEM((pieces_a, *(2,) * (steps - 1 - i), *tail_a), F32) for i in range(steps)],
            [pltpu.VMEM((pieces_b, *(2,) * (steps - 1 - i), *tail_b), F32) for i in range(steps)],
            pltpu.VMEM((pieces_a, batch_count - 1, rows_a, TILE), F32),
            pltpu.VMEM((pieces_b, batch_count, sub, padded), F32),
            pltpu.VMEM((pieces_b, batch_count - 1, sub, padded), F32),
        ]
        + [sems((2, max(pieces_a, pieces_b), steps))] * 2
        + [sems((pieces_b, scene_count // 2))] * 2
        + [sems((pieces_a, batch_count - 1))] * 2
        + [sems((pieces_b, batch_count - 1))] * 2
    )
    spread, slots = piece_orders(tok, scene_count)
    moves = [jnp.asarray(x, BF16) for x in (spread, spread.T, slots, slots.T)]
    grad_scale = float(tok * scene_count * batch_count) ** -0.5
    vmem, anywhere = pl.BlockSpec(memory_space=pltpu.VMEM), pl.BlockSpec(memory_space=pl.ANY)
    results = pl.pallas_call(
        functools.partial(block_kernel, grad_scale, orders_ab, batch_count, width // heads),
        in_specs=[vmem] * 3 + [anywhere] * 5 + [vmem] * 5,
        out_shape=(
            shape_of(tok, width),
            shape_of(tok, width),
            shape_of(rows_a, cols_a),
            shape_of(rows_b, cols_b),
        ),
        scratch_shapes=scratch,
        compiler_params=pltpu.CompilerParams(
            vmem_limit_bytes=VMEM_LIMIT, collective_id=0, has_side_effects=True
        ),
    )(local, offsets, conv_weight, w_up, w_down, w_qkv, w_out, cot, score_bias, *moves)
    return hand_over(results)


def shape_of(*dims):
    return jax.ShapeDtypeStruct(dims, F32)


def call(kernel, outs, scratch, flops):
    return pl.pallas_call(
        kernel,
        out_shape=outs,
        scratch_shapes=scratch,
        compiler_params=pltpu.CompilerParams(vmem_limit_bytes=VMEM_LIMIT),
        cost_estimate=pl.CostEstimate(flops=flops, bytes_accessed=4000000, transcendentals=0),
    )


def orders(tok, scene_count):
    per, count = GROUP // scene_count, tok // GROUP
    row = np.arange(tok)
    group, slot = row // GROUP, row % GROUP
    source = ((slot % per) * scene_count + slot // per) * count + group
    perm = np.zeros((tok, tok), np.float32)
    perm[row, source] = 1.0
    return perm


def on_device(tokens, nbr_offset, cotangent, conv_weight, w_qkv, w_out, score_bias, w_up, w_down):
    local = tokens[0]
    tok, width = local.shape
    hidden_width = w_up.shape[1]
    heads = score_bias.shape[0]
    scene_count = lax.axis_size("scene")
    batch_count = lax.axis_size("batch")
    if can_fuse(
        tok, width, width // heads, conv_weight.shape[0], hidden_width, scene_count, batch_count
    ):
        block_out, grad_mid, *grads = fused(
            scene_count, batch_count, local, nbr_offset, cotangent[0],
            conv_weight, w_qkv, w_out, score_bias, w_up, w_down,
        )
        return (block_out[None], grad_mid[None], *grads)
    forward = [(i, i + 1) for i in range(scene_count - 1)]
    backward = [(target, source) for source, target in forward]
    low = lax.ppermute(local[tok - HALO :], "scene", forward)
    high = lax.ppermute(local[:HALO], "scene", backward)
    first, normed = call(
        conv_kernel,
        (shape_of(tok, width), shape_of(tok, width)),
        [pltpu.VMEM((tok + 2 * HALO, 2 * width), BF16), pltpu.VMEM((tok, TILE), F32)],
        8 * 10**9,
    )(local, low, high, nbr_offset[:, 0, :], conv_weight)
    per, count = GROUP // scene_count, tok // GROUP
    blocks = normed.reshape(per, scene_count, count, width)
    arrived = lax.all_to_all(blocks, "scene", split_axis=1, concat_axis=1, tiled=True)
    perm = orders(tok, scene_count)
    bias = jnp.tile(score_bias, (1, 1, TILE // GROUP))
    mixed = call(
        functools.partial(attend_kernel, width // heads),
        shape_of(tok, width),
        [pltpu.VMEM((tok, 3 * width), F32), pltpu.VMEM((tok, width), F32)],
        10**10,
    )(
        arrived.reshape(tok, width),
        jnp.asarray(perm, BF16),
        jnp.asarray(perm.T, BF16),
        w_qkv,
        w_out,
        bias,
    )
    returned = lax.all_to_all(
        mixed.reshape(per, scene_count, count, width), "scene", split_axis=1, concat_axis=1, tiled=True
    ).reshape(tok, width)
    grad_scale = float(tok * scene_count * batch_count) ** -0.5
    block_out, grad_mid, grad_up, grad_down = call(
        functools.partial(mlp_kernel, grad_scale),
        (
            shape_of(tok, width),
            shape_of(tok, width),
            shape_of(width, hidden_width),
            shape_of(hidden_width, width),
        ),
        [pltpu.VMEM((tok, 3 * width), BF16)] * 2
        + [pltpu.VMEM((width, 3 * tok), BF16)] * 2
        + [pltpu.VMEM((tok, width), F32)],
        10**10,
    )(first, returned, cotangent[0], w_up, w_down)
    grads = []
    for grad in (grad_up, grad_down):
        part = lax.psum_scatter(grad, "scene", scatter_dimension=0, tiled=True)
        grads.append(lax.psum_scatter(part, "batch", scatter_dimension=1, tiled=True))
    return (block_out[None], grad_mid[None], *grads)


def solution(mesh):
    tokens = P("batch", "scene", None)
    return jax.shard_map(
        on_device,
        mesh=mesh,
        in_specs=(tokens, P(None, "batch", "scene"), tokens) + (P(),) * 6,
        out_specs=(tokens, tokens, P("scene", "batch"), P("scene", "batch")),
        check_vma=False,
    )
```

```python
import functools

import jax
import jax.numpy as jnp
import numpy as np
from jax import lax
from jax.experimental import pallas as pl
from jax.experimental.pallas import tpu as pltpu
from jax.sharding import PartitionSpec as P

GROUP = 32
HALO = 64
TILE = 128
F32 = jnp.float32
BF16 = jnp.bfloat16
MESH = pl.DeviceIdType.MESH
VMEM_LIMIT = 56 * 1024 * 1024


def split(x):
    hi = x.astype(BF16)
    return hi, (x - hi.astype(F32)).astype(BF16)


def left3(x, axis=1):
    hi, lo = split(x)
    return jnp.concatenate([hi, hi, lo], axis=axis)


def right3(x, axis=0):
    hi, lo = split(x)
    return jnp.concatenate([hi, lo, hi], axis=axis)


def dot(a, b):
    return lax.dot_general(a, b, (((1,), (0,)), ((), ())), preferred_element_type=F32)


def dot_t(a, b):
    return lax.dot_general(a, b, (((1,), (1,)), ((), ())), preferred_element_type=F32)


def norm_of(values):
    average = jnp.mean(values, axis=-1, keepdims=True)
    centered = values - average
    variance = jnp.mean(centered * centered, axis=-1, keepdims=True)
    scale = lax.rsqrt(variance + 1e-05)
    return centered * scale, scale


def conv_kernel(local_ref, low_ref, high_ref, offset_ref, weight_ref, first_ref, normed_ref, ext, off_t):
    tok, width = local_ref.shape
    taps = weight_ref.shape[0]
    for start, ref in ((0, low_ref), (HALO, local_ref), (HALO + tok, high_ref)):
        hi, lo = split(ref[...])
        ext[pl.ds(start, ref.shape[0]), :width] = hi
        ext[pl.ds(start, ref.shape[0]), width:] = lo
    for b in range(tok // TILE):
        piece = offset_ref[:, b * TILE : (b + 1) * TILE]
        piece = jnp.where(piece > HALO, 4 * TILE, piece).astype(F32)
        piece = jnp.concatenate([piece, jnp.zeros((TILE - taps, TILE), F32)], axis=0)
        off_t[b * TILE : (b + 1) * TILE, :] = piece.T
    span = TILE + 2 * HALO
    base = (
        lax.broadcasted_iota(jnp.int32, (TILE, span), 1)
        - lax.broadcasted_iota(jnp.int32, (TILE, span), 0)
        - HALO
    ).astype(F32)

    @pl.loop(0, tok // TILE)
    def _(b):
        row = pl.multiple_of(b * TILE, TILE)
        window = ext[pl.ds(row, span), :]
        offsets = off_t[pl.ds(row, TILE), :]
        total = local_ref[pl.ds(row, TILE), :]
        for a in range(taps):
            pick = jnp.where(base == offsets[:, a : a + 1], 1.0, 0.0).astype(BF16)
            found = dot(pick, window)
            total += (found[:, :width] + found[:, width:]) * weight_ref[a : a + 1, :]
        first_ref[pl.ds(row, TILE), :] = total
        normed_ref[pl.ds(row, TILE), :] = norm_of(total)[0]


def attend_kernel(head_dim, x_ref, perm_ref, back_ref, wqkv_ref, wout_ref, bias_ref, out_ref, qkv, att):
    tok, width = x_ref.shape
    hi, lo = split(x_ref[...])
    hi = dot(perm_ref[...], hi).astype(BF16)
    lo = dot(perm_ref[...], lo).astype(BF16)
    rows3 = jnp.concatenate([hi, hi, lo], axis=1)
    for part in range(3):
        qkv[:, part * width : (part + 1) * width] = dot(
            rows3, right3(wqkv_ref[:, part * width : (part + 1) * width])
        )
    per_lane = TILE // head_dim
    shape = (TILE, TILE)
    same = (lax.broadcasted_iota(jnp.int32, shape, 0) ^ lax.broadcasted_iota(jnp.int32, shape, 1)) < GROUP
    away = jnp.where(same, 0.0, -1e30)
    lane = lax.broadcasted_iota(jnp.int32, shape, 1)

    @pl.loop(0, tok // TILE)
    def _(b):
        row = pl.ds(pl.multiple_of(b * TILE, TILE), TILE)
        for part in range(width // TILE):
            at = part * TILE
            q = qkv[row, at : at + TILE] * (head_dim**-0.5)
            k = qkv[row, width + at : width + at + TILE]
            v = qkv[row, 2 * width + at : 2 * width + at + TILE]
            keys, values = [], []
            for h in range(per_lane):
                mine = (lane >= h * head_dim) & (lane < (h + 1) * head_dim)
                keys.append(right3(jnp.where(mine, k, 0.0), axis=1))
                values.append(jnp.concatenate(split(jnp.where(mine, v, 0.0)), axis=1))
            scores = dot_t(left3(q), jnp.concatenate(keys, axis=0))
            his, los = [], []
            for h in range(per_lane):
                bias = jnp.concatenate([bias_ref[part * per_lane + h]] * (TILE // GROUP), axis=0)
                s = scores[:, h * TILE : (h + 1) * TILE] + bias + away
                e = jnp.exp(s - jnp.max(s, axis=-1, keepdims=True))
                p = e / jnp.sum(e, axis=-1, keepdims=True)
                p_hi, p_lo = split(p)
                his.append(p_hi)
                los.append(p_lo)
            values = jnp.concatenate(values, axis=0)
            both = dot(jnp.concatenate(his, axis=1), values)
            rest = dot(jnp.concatenate(los, axis=1), values[:, :TILE])
            att[row, at : at + TILE] = both[:, :TILE] + both[:, TILE:] + rest

    hi, lo = split(att[...])
    hi = dot(back_ref[...], hi).astype(BF16)
    lo = dot(back_ref[...], lo).astype(BF16)
    out_ref[...] = dot(jnp.concatenate([hi, hi, lo], axis=1), right3(wout_ref[...]))


def mlp_kernel(
    grad_scale, first_ref, mixed_ref, cot_ref, up_ref, down_ref,
    out_ref, mid_ref, gup_ref, gdown_ref,
    n_left, c_left, nt_left, ct_left, grad_normed,
):
    tok, width = first_ref.shape
    hidden_width = up_ref.shape[1]
    chunk = 2 * TILE
    middle = first_ref[...] + mixed_ref[...]
    normed, scale = norm_of(middle)
    cot = cot_ref[...]
    n_left[...] = left3(normed)
    c_left[...] = left3(cot)
    nt_left[...] = left3(normed.T * grad_scale)
    ct_left[...] = left3(cot.T * grad_scale)
    out_ref[...] = middle
    grad_normed[...] = jnp.zeros_like(grad_normed)

    @pl.loop(0, hidden_width // chunk)
    def _(c):
        at = pl.ds(pl.multiple_of(c * chunk, chunk), chunk)
        up_hi, up_lo = split(up_ref[:, at])
        down_hi, down_lo = split(down_ref[at, :])
        hidden = dot(n_left[...], jnp.concatenate([up_hi, up_lo, up_hi], axis=0))
        grad_act = dot_t(c_left[...], jnp.concatenate([down_hi, down_lo, down_hi], axis=1))
        cdf = 0.5 * (1.0 + lax.erf(hidden * (0.5**0.5)))
        act = hidden * cdf
        density = jnp.exp(-0.5 * hidden * hidden) * ((2.0 * np.pi) ** -0.5)
        grad_hidden = grad_act * (cdf + hidden * density)
        act_hi, act_lo = split(act)
        gh_hi, gh_lo = split(grad_hidden)
        gup_ref[:, at] = dot(nt_left[...], jnp.concatenate([gh_hi, gh_lo, gh_hi], axis=0))
        gdown_ref[at, :] = dot(ct_left[...], jnp.concatenate([act_hi, act_lo, act_hi], axis=0)).T
        out_ref[...] += dot(
            jnp.concatenate([act_hi, act_hi, act_lo], axis=1),
            jnp.concatenate([down_hi, down_lo, down_hi], axis=0),
        )
        grad_normed[...] += dot_t(
            jnp.concatenate([gh_hi, gh_hi, gh_lo], axis=1),
            jnp.concatenate([up_hi, up_lo, up_hi], axis=1),
        )

    g = grad_normed[...]
    along = jnp.mean(g * normed, axis=-1, keepdims=True)
    mid_ref[...] = cot + scale * (g - jnp.mean(g, axis=-1, keepdims=True) - normed * along)


def bits_of(index, order):
    return tuple((index >> bit) & 1 for bit in order)


def block_kernel(
    grad_scale, orders_ab, batch_count, head_dim,
    local_ref, offset_ref, weight_ref, up_hbm, down_hbm, qkv_hbm, wout_hbm, cot_hbm, bias_ref,
    spread_ref, gather_ref, slots_ref, unslots_ref,
    out_ref, mid_ref, gup_ref, gdown_ref,
    up_ref, down_ref, wqkv_ref, wout_ref, cot_ref, load_sem,
    low, high, halo_send, halo_recv, ext, off_t, first_ref,
    x_send, x_recv, y_send, y_recv, xs_sem, xr_sem, ys_sem, yr_sem,
    wqkv3, wout3, bias_tile, up_hi, up_lo, down_hi, down_lo,
    n_left, c_left, nt_left, ct_left, slope, act_hi, act_lo, gh_hi, gh_lo,
    acc_a, acc_b, recv_a, recv_b, zrecv_a, zsend_b, zrecv_b,
    send_sem, recv_sem, core_send, core_recv, za_send, za_recv, zb_send, zb_recv,
):
    tok, width = local_ref.shape
    hidden_width = up_ref.shape[1]
    steps = len(orders_ab[0])
    scene_count = 2**steps
    rows_a, rows_b = width // scene_count, hidden_width // scene_count
    cols_a, cols_b = hidden_width // batch_count, width // batch_count
    pieces_a, pieces_b = cols_a // TILE, width // TILE
    tiles = tok // TILE
    me, my_batch = lax.axis_index("scene"), lax.axis_index("batch")
    values = [(me // 2**bit) % 2 for bit in range(steps)]
    partners = [me + (1 - 2 * values[bit]) * 2**bit for bit in range(steps)]
    others = [lax.rem(my_batch + d, batch_count) for d in range(1, batch_count)]
    scenes = [lax.rem(me + d, scene_count) for d in range(1, scene_count)]

    barrier = pltpu.get_barrier_semaphore()
    for other in scenes:
        pl.semaphore_signal(barrier, inc=1, device_id={"scene": other}, device_id_type=MESH)
    for other in others:
        pl.semaphore_signal(barrier, inc=1, device_id={"batch": other}, device_id_type=MESH)
    loads = [
        pltpu.make_async_copy(source, target, load_sem.at[i])
        for i, (source, target) in enumerate(
            (
                (qkv_hbm, wqkv_ref),
                (wout_hbm, wout_ref),
                (cot_hbm, cot_ref),
                (up_hbm, up_ref),
                (down_hbm, down_ref),
            )
        )
    ]
    for load in loads:
        load.start()

    sent = []

    def start(copy):
        copy.start()
        sent.append(copy)

    def to_scene(source, target, send, recv, other):
        return pltpu.make_async_remote_copy(
            src_ref=source,
            dst_ref=target,
            send_sem=send,
            recv_sem=recv,
            device_id={"scene": other},
            device_id_type=MESH,
        )

    halo = [
        to_scene(local_ref.at[pl.ds(tok - HALO, HALO)], low, halo_send.at[0], halo_recv.at[0], scenes[0]),
        to_scene(local_ref.at[pl.ds(0, HALO)], high, halo_send.at[1], halo_recv.at[1], scenes[-1]),
    ]
    taps = weight_ref.shape[0]
    span = TILE + 2 * HALO

    def extend(row, block):
        hi, lo = split(block)
        ext[pl.ds(row, block.shape[0]), :width] = hi
        ext[pl.ds(row, block.shape[0]), width:] = lo

    extend(HALO, local_ref[...])
    for t in range(tiles):
        piece = offset_ref[:, 0, t * TILE : (t + 1) * TILE]
        piece = jnp.where(piece > HALO, 4 * TILE, piece).astype(F32)
        piece = jnp.concatenate([piece, jnp.zeros((TILE - taps, TILE), F32)], axis=0)
        off_t[t * TILE : (t + 1) * TILE, :] = piece.T
    for h in range(bias_ref.shape[0]):
        bias_tile[h] = jnp.concatenate([bias_ref[h]] * (TILE // GROUP), axis=1)
    pl.semaphore_wait(barrier, scene_count + batch_count - 2)
    for copy in halo:
        start(copy)
    base = (
        lax.broadcasted_iota(jnp.int32, (TILE, span), 1)
        - lax.broadcasted_iota(jnp.int32, (TILE, span), 0)
        - HALO
    ).astype(F32)

    def convolve(t):
        row = pl.multiple_of(t * TILE, TILE)
        window = ext[pl.ds(row, span), :]
        offsets = off_t[pl.ds(row, TILE), :]
        total = local_ref[pl.ds(row, TILE), :]
        for a in range(taps):
            pick = jnp.where(base == offsets[:, a : a + 1], 1.0, 0.0).astype(BF16)
            found = dot(pick, window)
            total += (found[:, :width] + found[:, width:]) * weight_ref[a : a + 1, :]
        first_ref[pl.ds(row, TILE), :] = total

    pl.loop(1, tiles - 1)(convolve)
    for copy in halo:
        copy.wait_recv()
    extend(0, jnp.where(me == 0, 0.0, low[...]))
    extend(HALO + tok, jnp.where(me == scene_count - 1, 0.0, high[...]))
    pl.loop(0, 2)(lambda j: convolve(j * (tiles - 1)))

    def move(matrix, rows):
        hi, lo = split(rows)
        return dot(matrix, hi), dot(matrix, lo)

    piece_rows = TILE // scene_count
    hi, lo = move(spread_ref[...], norm_of(first_ref[...])[0])
    x_send[...] = (hi + lo).reshape(x_send.shape)

    def exchange(source, target, t, d, send, recv):
        return to_scene(
            source.at[t, scenes[d]], target.at[t, me], send.at[t, d], recv.at[t, d], scenes[d]
        )

    for t in range(tiles):
        for d in range(scene_count - 1):
            start(exchange(x_send, x_recv, t, d, xs_sem, xr_sem))
        x_recv[t, me] = x_send[t, me]

    loads[0].wait()
    for part in range(3):
        at = slice(part * width, (part + 1) * width)
        wqkv3[:, at] = right3(wqkv_ref[:, at])
    loads[1].wait()
    wout3[...] = right3(wout_ref[...])
    shape = (TILE, TILE)
    same = (lax.broadcasted_iota(jnp.int32, shape, 0) ^ lax.broadcasted_iota(jnp.int32, shape, 1)) < GROUP
    away = jnp.where(same, 0.0, -1e30)
    lane = lax.broadcasted_iota(jnp.int32, shape, 1)
    per_lane = TILE // head_dim

    def attend(qkv, part):
        at = part * TILE
        q = qkv[:, at : at + TILE] * (head_dim**-0.5)
        k = qkv[:, width + at : width + at + TILE]
        v = qkv[:, 2 * width + at : 2 * width + at + TILE]
        keys, vals = [], []
        for h in range(per_lane):
            mine = (lane >= h * head_dim) & (lane < (h + 1) * head_dim)
            keys.append(right3(jnp.where(mine, k, 0.0), axis=1))
            vals.append(jnp.concatenate(split(jnp.where(mine, v, 0.0)), axis=1))
        scores = dot_t(left3(q), jnp.concatenate(keys, axis=0))
        his, los = [], []
        for h in range(per_lane):
            bias = jnp.concatenate([bias_tile[part * per_lane + h]] * (TILE // GROUP), axis=0)
            s = scores[:, h * TILE : (h + 1) * TILE] + bias + away
            e = jnp.exp(s - jnp.max(s, axis=-1, keepdims=True))
            p_hi, p_lo = split(e / jnp.sum(e, axis=-1, keepdims=True))
            his.append(p_hi)
            los.append(p_lo)
        vals = jnp.concatenate(vals, axis=0)
        both = dot(jnp.concatenate(his, axis=1), vals)
        rest = dot(jnp.concatenate(los, axis=1), vals[:, :TILE])
        return both[:, :TILE] + both[:, TILE:] + rest

    for t in range(tiles):
        for d in range(scene_count - 1):
            exchange(x_send, x_recv, t, d, xs_sem, xr_sem).wait_recv()
        hi, lo = move(slots_ref[...], x_recv[t].reshape(TILE, width))
        hi, lo = hi.astype(BF16), lo.astype(BF16)
        qkv = dot(jnp.concatenate([hi, hi, lo], axis=1), wqkv3[...])
        att = jnp.concatenate([attend(qkv, part) for part in range(width // TILE)], axis=1)
        hi, lo = move(unslots_ref[...], att)
        hi, lo = hi.astype(BF16), lo.astype(BF16)
        mixed = dot(jnp.concatenate([hi, hi, lo], axis=1), wout3[...])
        y_send[t] = mixed.reshape(scene_count, piece_rows, width)
        for d in range(scene_count - 1):
            start(exchange(y_send, y_recv, t, d, ys_sem, yr_sem))
        y_recv[t, me] = y_send[t, me]

    loads[2].wait()
    cot = cot_ref[...]
    c_left[...] = left3(cot)
    cot_t = cot.T * grad_scale
    sub = TILE // batch_count
    ct_left[...] = left3(
        jnp.concatenate(
            [
                cot_t[b * cols_b + q * sub : b * cols_b + (q + 1) * sub]
                for q in range(pieces_b)
                for b in range(batch_count)
            ],
            axis=0,
        )
    )
    for load, source, hi_ref, lo_ref in ((loads[3], up_ref, up_hi, up_lo), (loads[4], down_ref, down_hi, down_lo)):
        load.wait()
        hi, lo = split(source[...])
        hi_ref[...] = hi
        lo_ref[...] = lo

    accs, recvs = (acc_a, acc_b), (recv_a, recv_b)

    def kept(stream, upto):
        return tuple(values[bit] for bit in orders_ab[stream][:upto])

    def halving(stream, q, i):
        bit = orders_ab[stream][i]
        return to_scene(
            accs[stream].at[(q, *kept(stream, i), 1 - values[bit])],
            recvs[stream][i].at[q],
            send_sem.at[stream, q, i],
            recv_sem.at[stream, q, i],
            partners[bit],
        )

    def to_batch(stream, q, d):
        send, recv = ((za_send, za_recv), (zb_send, zb_recv))[stream]
        source = acc_a.at[(q, *kept(0, steps), others[d])] if stream == 0 else zsend_b.at[q, others[d]]
        return pltpu.make_async_remote_copy(
            src_ref=source,
            dst_ref=(zrecv_a, zrecv_b)[stream].at[q, d],
            send_sem=send.at[q, d],
            recv_sem=recv.at[q, d],
            device_id={"batch": others[d]},
            device_id_type=MESH,
        )

    done = set()

    def advance(stream, q, i):
        if (stream, q, i) in done:
            return
        done.add((stream, q, i))
        halving(stream, q, i).wait_recv()
        mine = (q, *kept(stream, i + 1))
        accs[stream][mine] = accs[stream][mine] + recvs[stream][i][q]
        if i + 1 < steps:
            start(halving(stream, q, i + 1))
            return
        if stream == 1:
            pad = jnp.zeros((zsend_b.shape[-1] - rows_b, TILE), F32)
            whole = jnp.concatenate([acc_b[mine], pad], axis=0)
            zsend_b[q] = whole.T.reshape(zsend_b.shape[1:])
        for d in range(batch_count - 1):
            start(to_batch(stream, q, d))

    for t in range(tiles):
        for d in range(scene_count - 1):
            exchange(y_send, y_recv, t, d, ys_sem, yr_sem).wait_recv()
    hi, lo = move(gather_ref[...], y_recv[...].reshape(tok, width))
    middle = first_ref[...] + (hi + lo)
    normed, scale = norm_of(middle)
    n_left[...] = left3(normed)

    chunk = 2 * rows_b
    chunks = hidden_width // chunk
    top = values[steps - 1]

    def chunk_at(j):
        return lax.rem((1 - top) * (chunks // 2) + j, chunks)

    def chunk_bits(j):
        return tuple((chunk_at(j) // 2 ** (bit - 1)) % 2 for bit in orders_ab[1][1:])

    def early(q, j):
        return to_scene(
            acc_b.at[(q, 1 - values[0], *chunk_bits(j))],
            recv_b[0].at[(q, *chunk_bits(j))],
            core_send.at[q, j],
            core_recv.at[q, j],
            partners[0],
        )

    def add_early(q, half):
        for j in range(half * (chunks // 2), (half + 1) * (chunks // 2)):
            early(q, j).wait_recv()
        which = (1 - top, top)[half]
        acc_b[q, values[0], which] = acc_b[q, values[0], which] + recv_b[0][q, which]
        if half == 0:
            start(halving(1, q, 1))

    for j in range(chunks):
        at = pl.ds(pl.multiple_of(chunk_at(j) * chunk, chunk), chunk)
        hidden = dot(n_left[...], jnp.concatenate([up_hi[:, at], up_lo[:, at], up_hi[:, at]], axis=0))
        cdf = 0.5 * (1.0 + lax.erf(hidden * (0.5**0.5)))
        density = jnp.exp(-0.5 * hidden * hidden) * ((2.0 * np.pi) ** -0.5)
        slope[:, at] = cdf + hidden * density
        hi, lo = split(hidden * cdf)
        act_hi[:, at] = hi
        act_lo[:, at] = lo
        grad = dot(ct_left[...], jnp.concatenate([hi, lo, hi], axis=0)).T
        for half in range(2):
            for q in range(pieces_b):
                acc_b[(q, half, *chunk_bits(j))] = grad[
                    half * rows_b : (half + 1) * rows_b, q * TILE : (q + 1) * TILE
                ]
        for q in range(pieces_b):
            start(early(q, j))
        if j >= chunks // 2 and j - chunks // 2 < pieces_b:
            add_early(j - chunks // 2, 0)
    nt_left[...] = left3(normed.T * grad_scale)

    part = batch_count * TILE
    wheres = [
        [slice(b * cols_a + q * TILE, b * cols_a + (q + 1) * TILE) for b in range(batch_count)]
        for q in range(pieces_a)
    ]
    for q in range(pieces_a):
        d_hi = jnp.concatenate([down_hi[w, :] for w in wheres[q]], axis=0)
        d_lo = jnp.concatenate([down_lo[w, :] for w in wheres[q]], axis=0)
        grad_act = dot_t(c_left[...], jnp.concatenate([d_hi, d_lo, d_hi], axis=1))
        hi, lo = split(grad_act * jnp.concatenate([slope[:, w] for w in wheres[q]], axis=1))
        gh_hi[:, q * part : (q + 1) * part] = hi
        gh_lo[:, q * part : (q + 1) * part] = lo
        grad = dot(nt_left[...], jnp.concatenate([hi, lo, hi], axis=0))
        for s in range(scene_count):
            for b in range(batch_count):
                acc_a[(q, *bits_of(s, orders_ab[0]), b)] = grad[
                    s * rows_a : (s + 1) * rows_a, b * TILE : (b + 1) * TILE
                ]
        start(halving(0, q, 0))
        if q == 0:
            for p in range(min(chunks // 2 + chunks % 2, pieces_b), pieces_b):
                add_early(p, 0)
            for p in range(pieces_b):
                add_early(p, 1)
        else:
            advance(0, q - 1, 0)
        if q == 1:
            advance(1, 0, 1)

    out_ref[...] = (
        middle
        + dot(act_hi[...], down_hi[...])
        + dot(act_hi[...], down_lo[...])
        + dot(act_lo[...], down_hi[...])
    )
    advance(0, pieces_a - 1, 0)
    for p in range(pieces_b - 1):
        advance(1, p, 1)
    advance(0, 0, 1)

    g = jnp.zeros((tok, width), F32)
    for q in range(pieces_a):
        u_hi = jnp.concatenate([up_hi[:, w] for w in wheres[q]], axis=1)
        u_lo = jnp.concatenate([up_lo[:, w] for w in wheres[q]], axis=1)
        hi, lo = gh_hi[:, q * part : (q + 1) * part], gh_lo[:, q * part : (q + 1) * part]
        g += dot_t(hi, u_hi) + dot_t(hi, u_lo) + dot_t(lo, u_hi)
    along = jnp.mean(g * normed, axis=-1, keepdims=True)
    mid_ref[...] = cot_ref[...] + scale * (g - jnp.mean(g, axis=-1, keepdims=True) - normed * along)

    advance(1, pieces_b - 1, 1)
    if pieces_a > 2:
        advance(0, 1, 1)
    for i in range(1, steps):
        for q in range(max(pieces_a, pieces_b)):
            for stream, count in ((1, pieces_b), (0, pieces_a)):
                if q < count:
                    advance(stream, q, i)
    rows = []
    for q in range(pieces_b):
        total = zsend_b[q, my_batch]
        for d in range(batch_count - 1):
            to_batch(1, q, d).wait_recv()
            total += zrecv_b[q, d]
        rows.append(total)
    rows.append(jnp.zeros((TILE - cols_b, rows[0].shape[1]), F32))
    gdown_ref[...] = jnp.concatenate(rows, axis=0).T[:rows_b, :cols_b]
    for q in range(pieces_a):
        total = acc_a[(q, *kept(0, steps), my_batch)]
        for d in range(batch_count - 1):
            to_batch(0, q, d).wait_recv()
            total += zrecv_a[q, d]
        gup_ref[:, q * TILE : (q + 1) * TILE] = total
    for copy in sent:
        copy.wait_send()


def can_fuse(tok, width, head_dim, taps, hidden_width, scene_count, batch_count):
    return (
        scene_count >= 4
        and scene_count & (scene_count - 1) == 0
        and GROUP % scene_count == 0
        and (TILE // scene_count) % 8 == 0
        and batch_count > 1
        and tok % TILE == 0
        and tok // TILE > 1
        and width % TILE == 0
        and TILE % head_dim == 0
        and taps <= TILE
        and TILE % (8 * batch_count) == 0
        and (width // scene_count) % 8 == 0
        and (hidden_width // scene_count) % 64 == 0
        and (hidden_width // batch_count) % TILE == 0
        and width // batch_count < TILE
    )


def piece_orders(tok, scene_count):
    per, count, some = GROUP // scene_count, tok // GROUP, TILE // GROUP
    row = np.arange(tok)
    tile, rest = row // TILE, row % TILE
    device, k, g = rest // (per * some), rest // some % per, rest % some
    spread = np.zeros((tok, tok), np.float32)
    spread[row, (k * scene_count + device) * count + tile * some + g] = 1.0
    row = np.arange(TILE)
    slots = np.zeros((TILE, TILE), np.float32)
    slots[row, row % GROUP * some + row // GROUP] = 1.0
    return spread, slots


def hand_over_kernel(*refs):
    for source, target in zip(refs[:4], refs[4:]):
        target[...] = source[...]


def hand_over(results):
    return pl.pallas_call(
        hand_over_kernel,
        out_shape=tuple(shape_of(*x.shape) for x in results),
        compiler_params=pltpu.CompilerParams(vmem_limit_bytes=VMEM_LIMIT),
    )(*results)


def fused(scene_count, batch_count, local, offsets, cot, conv_weight, w_qkv, w_out, score_bias, w_up, w_down):
    tok, width = local.shape
    hidden_width = w_up.shape[1]
    heads = score_bias.shape[0]
    steps = scene_count.bit_length() - 1
    orders_ab = (tuple(range(steps)), (0, *reversed(range(1, steps))))
    rows_a, rows_b = width // scene_count, hidden_width // scene_count
    cols_a = hidden_width // batch_count
    cols_b = width // batch_count
    pieces_a, pieces_b = cols_a // TILE, width // TILE
    tail_a, tail_b = (batch_count, rows_a, TILE), (rows_b, TILE)
    padded = -(-rows_b // TILE) * TILE
    sub = TILE // batch_count
    tiles = tok // TILE
    sems = pltpu.SemaphoreType.DMA
    scratch = (
        [pltpu.VMEM(x.shape, F32) for x in (w_up, w_down, w_qkv, w_out, cot)]
        + [sems((5,))]
        + [pltpu.VMEM((HALO, width), F32)] * 2
        + [sems((2,))] * 2
        + [
            pltpu.VMEM((tok + 2 * HALO, 2 * width), BF16),
            pltpu.VMEM((tok, TILE), F32),
            pltpu.VMEM((tok, width), F32),
        ]
        + [pltpu.VMEM((tiles, scene_count, TILE // scene_count, width), F32)] * 4
        + [sems((tiles, scene_count - 1))] * 4
        + [
            pltpu.VMEM((3 * width, 3 * width), BF16),
            pltpu.VMEM((3 * width, width), BF16),
            pltpu.VMEM((heads, GROUP, TILE), F32),
        ]
        + [pltpu.VMEM(w_up.shape, BF16)] * 2
        + [pltpu.VMEM(w_down.shape, BF16)] * 2
        + [pltpu.VMEM((tok, 3 * width), BF16)] * 2
        + [pltpu.VMEM((width, 3 * tok), BF16)] * 2
        + [pltpu.VMEM((tok, hidden_width), F32)]
        + [pltpu.VMEM((tok, hidden_width), BF16)] * 4
        + [
            pltpu.VMEM((pieces_a, *(2,) * steps, *tail_a), F32),
            pltpu.VMEM((pieces_b, *(2,) * steps, *tail_b), F32),
            [pltpu.VMEM((pieces_a, *(2,) * (steps - 1 - i), *tail_a), F32) for i in range(steps)],
            [pltpu.VMEM((pieces_b, *(2,) * (steps - 1 - i), *tail_b), F32) for i in range(steps)],
            pltpu.VMEM((pieces_a, batch_count - 1, rows_a, TILE), F32),
            pltpu.VMEM((pieces_b, batch_count, sub, padded), F32),
            pltpu.VMEM((pieces_b, batch_count - 1, sub, padded), F32),
        ]
        + [sems((2, max(pieces_a, pieces_b), steps))] * 2
        + [sems((pieces_b, scene_count // 2))] * 2
        + [sems((pieces_a, batch_count - 1))] * 2
        + [sems((pieces_b, batch_count - 1))] * 2
    )
    spread, slots = piece_orders(tok, scene_count)
    moves = [jnp.asarray(x, BF16) for x in (spread, spread.T, slots, slots.T)]
    grad_scale = float(tok * scene_count * batch_count) ** -0.5
    vmem, anywhere = pl.BlockSpec(memory_space=pltpu.VMEM), pl.BlockSpec(memory_space=pl.ANY)
    results = pl.pallas_call(
        functools.partial(block_kernel, grad_scale, orders_ab, batch_count, width // heads),
        in_specs=[vmem] * 3 + [anywhere] * 5 + [vmem] * 5,
        out_shape=(
            shape_of(tok, width),
            shape_of(tok, width),
            shape_of(rows_a, cols_a),
            shape_of(rows_b, cols_b),
        ),
        scratch_shapes=scratch,
        compiler_params=pltpu.CompilerParams(
            vmem_limit_bytes=VMEM_LIMIT, collective_id=0, has_side_effects=True
        ),
    )(local, offsets, conv_weight, w_up, w_down, w_qkv, w_out, cot, score_bias, *moves)
    return hand_over(results)


def shape_of(*dims):
    return jax.ShapeDtypeStruct(dims, F32)


def call(kernel, outs, scratch, flops):
    return pl.pallas_call(
        kernel,
        out_shape=outs,
        scratch_shapes=scratch,
        compiler_params=pltpu.CompilerParams(vmem_limit_bytes=VMEM_LIMIT),
        cost_estimate=pl.CostEstimate(flops=flops, bytes_accessed=4000000, transcendentals=0),
    )


def orders(tok, scene_count):
    per, count = GROUP // scene_count, tok // GROUP
    row = np.arange(tok)
    group, slot = row // GROUP, row % GROUP
    source = ((slot % per) * scene_count + slot // per) * count + group
    perm = np.zeros((tok, tok), np.float32)
    perm[row, source] = 1.0
    return perm


def on_device(tokens, nbr_offset, cotangent, conv_weight, w_qkv, w_out, score_bias, w_up, w_down):
    local = tokens[0]
    tok, width = local.shape
    hidden_width = w_up.shape[1]
    heads = score_bias.shape[0]
    scene_count = lax.axis_size("scene")
    batch_count = lax.axis_size("batch")
    if can_fuse(
        tok, width, width // heads, conv_weight.shape[0], hidden_width, scene_count, batch_count
    ):
        block_out, grad_mid, *grads = fused(
            scene_count, batch_count, local, nbr_offset, cotangent[0],
            conv_weight, w_qkv, w_out, score_bias, w_up, w_down,
        )
        return (block_out[None], grad_mid[None], *grads)
    forward = [(i, i + 1) for i in range(scene_count - 1)]
    backward = [(target, source) for source, target in forward]
    low = lax.ppermute(local[tok - HALO :], "scene", forward)
    high = lax.ppermute(local[:HALO], "scene", backward)
    first, normed = call(
        conv_kernel,
        (shape_of(tok, width), shape_of(tok, width)),
        [pltpu.VMEM((tok + 2 * HALO, 2 * width), BF16), pltpu.VMEM((tok, TILE), F32)],
        8 * 10**9,
    )(local, low, high, nbr_offset[:, 0, :], conv_weight)
    per, count = GROUP // scene_count, tok // GROUP
    blocks = normed.reshape(per, scene_count, count, width)
    arrived = lax.all_to_all(blocks, "scene", split_axis=1, concat_axis=1, tiled=True)
    perm = orders(tok, scene_count)
    bias = jnp.tile(score_bias, (1, 1, TILE // GROUP))
    mixed = call(
        functools.partial(attend_kernel, width // heads),
        shape_of(tok, width),
        [pltpu.VMEM((tok, 3 * width), F32), pltpu.VMEM((tok, width), F32)],
        10**10,
    )(
        arrived.reshape(tok, width),
        jnp.asarray(perm, BF16),
        jnp.asarray(perm.T, BF16),
        w_qkv,
        w_out,
        bias,
    )
    returned = lax.all_to_all(
        mixed.reshape(per, scene_count, count, width), "scene", split_axis=1, concat_axis=1, tiled=True
    ).reshape(tok, width)
    grad_scale = float(tok * scene_count * batch_count) ** -0.5
    block_out, grad_mid, grad_up, grad_down = call(
        functools.partial(mlp_kernel, grad_scale),
        (
            shape_of(tok, width),
            shape_of(tok, width),
            shape_of(width, hidden_width),
            shape_of(hidden_width, width),
        ),
        [pltpu.VMEM((tok, 3 * width), BF16)] * 2
        + [pltpu.VMEM((width, 3 * tok), BF16)] * 2
        + [pltpu.VMEM((tok, width), F32)],
        10**10,
    )(first, returned, cotangent[0], w_up, w_down)
    grads = []
    for grad in (grad_up, grad_down):
        part = lax.psum_scatter(grad, "scene", scatter_dimension=0, tiled=True)
        grads.append(lax.psum_scatter(part, "batch", scatter_dimension=1, tiled=True))
    return (block_out[None], grad_mid[None], *grads)


def solution(mesh):
    tokens = P("batch", "scene", None)
    return jax.shard_map(
        on_device,
        mesh=mesh,
        in_specs=(tokens, P(None, "batch", "scene"), tokens) + (P(),) * 6,
        out_specs=(tokens, tokens, P("scene", "batch"), P("scene", "batch")),
        check_vma=False,
    )
```
